128 devices in a mesh: dp: 2 (over core), ctx: 64 (over z, y, x).
Axes of the slice: x: 4, y: 4, z: 4, core: 2. Of those that a mesh axis runs over, the one named last changes fastest.
Arguments:
- layer_in: bfloat16 [2, 8192, 576], P('dp', 'ctx'), may hold values from -6 to 6
- positions: int32 [2, 8192], P('dp', 'ctx'), may hold values from 0 to 24575, as said below
- norm_gain1: bfloat16 [576], P('dp'), may hold values from 0.25 to 1.75
- w_query: bfloat16 [576, 576], P('dp'), may hold values from -0.25 to 0.25
- w_key: bfloat16 [576, 192], P('dp'), may hold values from -0.25 to 0.25
- w_value: bfloat16 [576, 192], P('dp'), may hold values from -0.25 to 0.25
- w_out: bfloat16 [576, 576], P('dp'), may hold values from -1.5 to 1.5
- norm_gain2: bfloat16 [576], P('dp'), may hold values from 0.25 to 1.75
- w_gate: bfloat16 [576, 1536], P('dp'), may hold values from -0.25 to 0.25
- w_up: bfloat16 [576, 1536], P('dp'), may hold values from -0.25 to 0.25
- w_down: bfloat16 [1536, 576], P('dp'), may hold values from -0.15625 to 0.15625
- cotangent: bfloat16 [2, 8192, 576], P('dp', 'ctx'), may hold values from -6 to 6
Outputs:
- layer_out: bfloat16 [2, 8192, 576], P('dp', 'ctx')
- input_grad: bfloat16 [2, 8192, 576], P('dp', 'ctx')
- grad_gain1: float32 [576], P('dp')
- grad_query: float32 [576, 576], P('dp')
- grad_key: float32 [576, 192], P('dp')
- grad_value: float32 [576, 192], P('dp')
- grad_out: float32 [576, 576], P('dp')
- grad_gain2: float32 [576], P('dp')
- grad_gate: float32 [576, 1536], P('dp')
- grad_up: float32 [576, 1536], P('dp')
- grad_down: float32 [1536, 576], P('dp')
The draws below stay inside these ranges and needn't reach their ends.
Inputs may be any that keep to these rules, and one draw needn't show every extreme that they name: Along each sequence the positions rise by 1 or 2 from one token to the next.
All inputs are finite; a program needn't handle non-finite values.
Results may differ from the reference program's by a relative error of at most 0.022.
Values may be sent and summed in bfloat16 or wider, within the bound.
A program may use at most 128 MiB of HBM per device.

```python
import jax
import jax.numpy as jnp
from jax import lax

D = 576
HEADS = 9
KV_HEADS = 3
HEAD = 64
FF = 1536
SEQ = 8192
SEQS = 2


def draw_positions(key, part):
    key = jax.random.fold_in(key, 7)
    first_key, second_key = jax.random.split(key)
    strides = jax.random.randint(second_key, (SEQS, SEQ), 1, 3).astype(jnp.int32)
    climb = (jnp.cumsum(strides, axis=1) - strides[:, :1]).astype(jnp.int32)
    room = 3 * SEQ - 1 - climb[:, -1:]
    drawn = jax.random.randint(first_key, (SEQS, 1), 0, room + 1).astype(jnp.int32)
    seq_ids = jnp.arange(SEQS, dtype=jnp.int32)[:, None]
    offsets = jnp.where(seq_ids == SEQS - 1, room, drawn)
    offsets = jnp.where(seq_ids == 0, jnp.zeros_like(drawn), offsets)
    return (offsets + climb).astype(jnp.int32)


def block_levels(key, extent, cuts, low, top_value):
    loudness, own = 1.0, jax.random.fold_in(key, 6)
    for position, shards_of in cuts:
        draws = jnp.exp(jax.random.uniform(jax.random.fold_in(own, position), (shards_of,), jnp.float32, low / len(cuts), top_value / len(cuts)))
        loudness = loudness * jnp.repeat(draws, extent[position] // shards_of).reshape([-1 if axis == position else 1 for axis in range(len(extent))])
    return loudness


def normal_values(rng, shape, spread, limit, cuts=(), kind=jnp.bfloat16):
    values = spread * jax.random.normal(rng, shape, jnp.float32)
    if cuts:
        values = values * block_levels(rng, shape, cuts, -0.22, 0.18)
    return jnp.clip(values, -limit, limit).astype(kind)


def setup_inputs(seed: int = 0) -> dict:
    arg_keys = jax.random.split(jax.random.key(seed), 13)
    return {
        "layer_in": normal_values(arg_keys[0], (SEQS, SEQ, D), 1.0, 6.0, ((0, 2), (1, 64))),
        "positions": draw_positions(jax.random.fold_in(arg_keys[12], 71), 0),
        "norm_gain1": jnp.clip(1.0 + 0.15 * jax.random.normal(arg_keys[2], (D,), jnp.float32), 0.25, 1.75).astype(jnp.bfloat16),
        "w_query": normal_values(arg_keys[3], (D, D), D ** -0.5, 0.25, ((0, 2),)),
        "w_key": normal_values(arg_keys[4], (D, KV_HEADS * HEAD), D ** -0.5, 0.25, ((0, 2),)),
        "w_value": normal_values(arg_keys[5], (D, KV_HEADS * HEAD), D ** -0.5, 0.25, ((0, 2),)),
        "w_out": normal_values(arg_keys[6], (D, D), (D // 32) ** -0.5, 1.5, ((0, 2),)),
        "norm_gain2": jnp.clip(1.0 + 0.15 * jax.random.normal(arg_keys[7], (D,), jnp.float32), 0.25, 1.75).astype(jnp.bfloat16),
        "w_gate": normal_values(arg_keys[8], (D, FF), D ** -0.5, 0.25, ((0, 2),)),
        "w_up": normal_values(arg_keys[9], (D, FF), D ** -0.5, 0.25, ((0, 2),)),
        "w_down": normal_values(arg_keys[10], (FF, D), FF ** -0.5, 0.15625, ((0, 2),)),
        "cotangent": normal_values(arg_keys[11], (SEQS, SEQ, D), 1.0, 6.0, ((0, 2), (1, 64))),
    }


EPS = 1e-05
MASKED = -1e+30
HIGH = lax.Precision.HIGHEST

@jax.custom_vjp
def low(v):
    return lax.optimization_barrier(v.astype(jnp.bfloat16)).astype(jnp.float32)

@jax.custom_vjp
def low_back(v):
    return v

def low_keep(v):
    return (low(v), None)

def low_pass(kept, grad):
    return (grad,)

def back_keep(v):
    return (v, None)

def back_low(kept, grad):
    return (low(grad),)
low.defvjp(low_keep, low_pass)
low_back.defvjp(back_keep, back_low)

def matmul(left, right):
    return jnp.dot(left, right, precision=HIGH)

def rms(values, gain):
    return values * lax.rsqrt(lax.optimization_barrier(jnp.mean(values * values, axis=-1, keepdims=True)) + EPS) * gain

def rotate(values, positions):
    half_dim = HEAD // 2
    inv_freq = 10000.0 ** (-jnp.arange(half_dim, dtype=jnp.float32) / half_dim)
    angles = positions.astype(jnp.float32)[:, None] * inv_freq[None, :]
    cosines = jnp.cos(angles)[:, None, :]
    sines = jnp.sin(angles)[:, None, :]
    first, second = jnp.split(values, 2, axis=-1)
    return jnp.concatenate([first * cosines - second * sines, second * cosines + first * sines], axis=-1)

def attend(queries, keys, values):
    seq = queries.shape[0]
    block = min(512, seq)
    count = seq // block
    groups = HEADS // KV_HEADS
    scale = HEAD ** (-0.5)
    q_blocks = queries.reshape(count, block, KV_HEADS, groups, HEAD)
    cols = jnp.arange(seq, dtype=jnp.int32)

    def one(args):
        q_block, index = args
        rows = index * block + jnp.arange(block, dtype=jnp.int32)
        scores = low_back(jnp.einsum('tkgd,pkd->kgtp', q_block, keys, precision=HIGH) * scale)
        scores = jnp.where(cols[None, :] <= rows[:, None], scores, MASKED)
        top = lax.optimization_barrier(jnp.max(scores, axis=-1, keepdims=True))
        weights = jnp.exp(scores - top)
        probs = low(weights / lax.optimization_barrier(jnp.sum(weights, axis=-1, keepdims=True)))
        return jnp.einsum('kgtp,pkd->tkgd', probs, values, precision=HIGH)
    outs = lax.map(jax.checkpoint(one), (q_blocks, jnp.arange(count, dtype=jnp.int32)))
    return outs.reshape(seq, HEADS * HEAD)

def layer(params, inputs, positions):
    gain1, wq, wk, wv, wo, gain2, wg, wu, wd = params
    results = []
    for index in range(inputs.shape[0]):
        x = inputs[index]
        pos = positions[index]
        seq = x.shape[0]
        h1 = low(rms(x, gain1))
        q_lin = low_back(matmul(h1, wq)).reshape(seq, HEADS, HEAD)
        k_lin = low_back(matmul(h1, wk)).reshape(seq, KV_HEADS, HEAD)
        vals = low(low_back(matmul(h1, wv))).reshape(seq, KV_HEADS, HEAD)
        queries = low(rotate(q_lin, pos))
        keys = low(rotate(k_lin, pos))
        attn = low(low_back(attend(queries, keys, vals)))
        x2 = x + low_back(matmul(attn, wo))
        h2 = low(rms(x2, gain2))
        gate = low_back(matmul(h2, wg))
        up = low_back(matmul(h2, wu))
        hidden = low(gate * jax.nn.sigmoid(gate) * up)
        results.append(x2 + low_back(matmul(hidden, wd)))
    return jnp.stack(results)

def reference(layer_in, positions, norm_gain1, w_query, w_key, w_value, w_out, norm_gain2, w_gate, w_up, w_down, cotangent):
    params = tuple((p.astype(jnp.float32) for p in (norm_gain1, w_query, w_key, w_value, w_out, norm_gain2, w_gate, w_up, w_down)))
    inputs = layer_in.astype(jnp.float32)
    result, pull = jax.vjp(lambda p, x: layer(p, x, positions), params, inputs)
    grads, grad_in = pull(cotangent.astype(jnp.float32))
    return (result.astype(jnp.bfloat16), grad_in.astype(jnp.bfloat16), grads[0], grads[1], grads[2], grads[3], grads[4], grads[5], grads[6], grads[7], grads[8])
```

```python
import jax
import jax.numpy as jnp
from jax import lax
from jax.experimental import pallas as pl
from jax.experimental.pallas import tpu as pltpu
from jax.sharding import PartitionSpec as P

HEADS = 9
KV_HEADS = 3
GROUPS = HEADS // KV_HEADS
HEAD = 64
D = 576
FF = 1536
EPS = 1e-05
MASKED = -1e30
HALF = 64
GROUP = 8
KEYS = GROUP * HALF
ROWS = 2 * HALF
MESH = pl.DeviceIdType.MESH
F32 = jnp.float32
BF16 = jnp.bfloat16
VMEM_LIMIT = 60 * 1024 * 1024

E_GATE = 0
E_UP = 12 * 288
E_DOWN = 24 * 288
E_OUT = E_DOWN + 5 * 768
E_GAIN = E_OUT + 5 * 288
E_ROWS = 3 * 64 * 64


def vmem(n):
    return [pl.BlockSpec(memory_space=pltpu.VMEM)] * n


def anywhere(n):
    return [pl.BlockSpec(memory_space=pl.ANY)] * n


def shape(dims, dtype):
    return jax.ShapeDtypeStruct(dims, dtype)


def nn(a, b):
    return jnp.dot(a, b, preferred_element_type=F32)


def nt(a, b):
    return lax.dot_general(a, b, (((1,), (1,)), ((), ())), preferred_element_type=F32)


def tn(a, b):
    return lax.dot_general(a, b, (((0,), (0,)), ((), ())), preferred_element_type=F32)


def run_together(*tasks):
    tasks = list(tasks)
    while tasks:
        for task in list(tasks):
            try:
                next(task)
            except StopIteration:
                tasks.remove(task)


class Place:
    def __init__(self):
        self.core = lax.axis_index("dp")
        self.me = lax.axis_index("ctx")
        self.at = [lax.rem(self.me // 4**a, 4) for a in range(3)]

    def toward(self, axis, step):
        there = lax.rem(self.at[axis] + step, 4)
        return self.me + (there - self.at[axis]) * 4**axis

    def coord(self, axis, step):
        return lax.rem(self.at[axis] + step, 4)

    def region(self, part, phase, coord):
        index = [None, None, None]
        for k in range(3):
            axis = (part + k) % 3
            index[2 - axis] = pl.ds(0, 4) if k < phase else coord if k == phase else self.at[axis]
        return tuple(index)


def send(src, dst, send_sem, recv_sem, device):
    copy = pltpu.make_async_remote_copy(
        src_ref=src, dst_ref=dst, send_sem=send_sem, recv_sem=recv_sem, device_id=device, device_id_type=MESH
    )
    copy.start()
    return copy


def arrived(dst, send_sem, recv_sem, device):
    pltpu.make_async_remote_copy(
        src_ref=dst, dst_ref=dst, send_sem=send_sem, recv_sem=recv_sem, device_id=device, device_id_type=MESH
    ).wait_recv()


def gather_task(place, buf, rows, ssem, rsem, done):
    first, second, whole = pl.ds(0, rows // 2), pl.ds(rows // 2, rows // 2), None
    sent = []
    for phase in range(3):
        for part in range(3):
            axis = (part + phase) % 3
            plus, minus = {"ctx": place.toward(axis, 1)}, {"ctx": place.toward(axis, 3)}
            own = place.region(part, phase, place.at[axis])
            for k, (half, to) in enumerate(((first, plus), (second, minus), (second, plus), (first, minus))):
                ref = buf.at[(part, *own, half)]
                sent.append(send(ref, ref, ssem.at[part, phase, k], rsem.at[part, phase, k], to))
        yield
        for part in range(3):
            axis = (part + phase) % 3
            plus, minus = {"ctx": place.toward(axis, 1)}, {"ctx": place.toward(axis, 3)}
            for k, (half, step, to) in enumerate(((first, 3, plus), (second, 1, minus))):
                ref = buf.at[(part, *place.region(part, phase, place.coord(axis, step)), half)]
                arrived(ref, ssem.at[part, phase, k], rsem.at[part, phase, k], to)
                sent.append(send(ref, ref, ssem.at[part, phase, 4 + k], rsem.at[part, phase, 4 + k], to))
        yield
        for part in range(3):
            axis = (part + phase) % 3
            plus = {"ctx": place.toward(axis, 1)}
            for k, half, step in ((2, second, 3), (3, first, 1), (4, first, 2), (5, second, 2)):
                ref = buf.at[(part, *place.region(part, phase, place.coord(axis, step)), half)]
                arrived(ref, ssem.at[part, phase, k], rsem.at[part, phase, k], plus)
        done(phase)
    yield
    for copy in sent:
        copy.wait_send()


def add_into(buf, index, other):
    buf[index] = (buf[index].astype(F32) + other.astype(F32)).astype(BF16)


def scatter_task(place, buf, halves, wholes, rows, ssem, rsem, finish):
    first, second = pl.ds(0, rows // 2), pl.ds(rows // 2, rows // 2)
    sent = []
    for turn in range(3):
        phase = 2 - turn
        half_buf, whole_buf = halves[turn], wholes[turn]
        for part in range(3):
            axis = (part + phase) % 3
            plus, minus = {"ctx": place.toward(axis, 1)}, {"ctx": place.toward(axis, 3)}
            far = place.region(part, phase, place.coord(axis, 2))
            right = place.region(part, phase, place.coord(axis, 1))
            left = place.region(part, phase, place.coord(axis, 3))
            lead = (slice(None),) * phase
            for k, src, dst, to in (
                (0, (*far, first), half_buf.at[part, 0], plus),
                (1, (*far, second), half_buf.at[part, 1], minus),
                (2, (*right, second), whole_buf.at[(part, 0, *lead, second)], plus),
                (3, (*left, first), whole_buf.at[(part, 1, *lead, first)], minus),
            ):
                sent.append(send(buf.at[(part, *src)], dst, ssem.at[part, turn, k], rsem.at[part, turn, k], to))
        yield
        for part in range(3):
            axis = (part + phase) % 3
            plus, minus = {"ctx": place.toward(axis, 1)}, {"ctx": place.toward(axis, 3)}
            lead = (slice(None),) * phase
            for k, half, step, to in ((0, first, 1, plus), (1, second, 3, minus)):
                arrived(half_buf.at[part, k], ssem.at[part, turn, k], rsem.at[part, turn, k], to)
                index = (part, *place.region(part, phase, place.coord(axis, step)), half)
                add_into(buf, index, half_buf[part, k])
                dst = whole_buf.at[(part, k, *lead, half)]
                sent.append(send(buf.at[index], dst, ssem.at[part, turn, 4 + k], rsem.at[part, turn, 4 + k], to))
        yield
        for part in range(3):
            axis = (part + phase) % 3
            plus = {"ctx": place.toward(axis, 1)}
            lead = (slice(None),) * phase
            for k, side, half in ((2, 0, second), (3, 1, first), (4, 0, first), (5, 1, second)):
                dst = whole_buf.at[(part, side, *lead, half)]
                arrived(dst, ssem.at[part, turn, k], rsem.at[part, turn, k], plus)
            index = (part, *place.region(part, phase, place.at[axis]))
            total = buf[index].astype(F32) + whole_buf[part, 0].astype(F32) + whole_buf[part, 1].astype(F32)
            if turn < 2:
                buf[index] = total.astype(BF16)
            else:
                finish(part, index, total)
    yield
    for copy in sent:
        copy.wait_send()


def small_sum_task(place, buf, slots, out, ssem, rsem, ssem2, rsem2):
    sent = []
    for turn in range(3):
        phase = 2 - turn
        for part in range(3):
            axis = (part + phase) % 3
            for k in range(3):
                src = buf.at[(part, *place.region(part, phase, place.coord(axis, k + 1)))]
                to = {"ctx": place.toward(axis, k + 1)}
                sent.append(send(src, slots[turn].at[part, k], ssem.at[part, turn, k], rsem.at[part, turn, k], to))
        yield
        for part in range(3):
            axis = (part + phase) % 3
            index = (part, *place.region(part, phase, place.at[axis]))
            total = buf[index].astype(F32)
            for k in range(3):
                to = {"ctx": place.toward(axis, k + 1)}
                arrived(slots[turn].at[part, k], ssem.at[part, turn, k], rsem.at[part, turn, k], to)
                total = total + slots[turn][part, k].astype(F32)
            if turn < 2:
                buf[index] = total.astype(BF16)
            else:
                out[index] = total.astype(BF16)
    for phase in range(3):
        for part in range(3):
            axis = (part + phase) % 3
            ref = out.at[(part, *place.region(part, phase, place.at[axis]))]
            for k in range(3):
                to = {"ctx": place.toward(axis, k + 1)}
                sent.append(send(ref, ref, ssem2.at[part, phase, k], rsem2.at[part, phase, k], to))
        yield
        for part in range(3):
            axis = (part + phase) % 3
            for k in range(3):
                to = {"ctx": place.toward(axis, k + 1)}
                ref = out.at[(part, *place.region(part, phase, place.coord(axis, 3 - k)))]
                arrived(ref, ssem2.at[part, phase, k], rsem2.at[part, phase, k], to)
    yield
    for copy in sent:
        copy.wait_send()


def greet(place, steps, callers, targets):
    barrier = pltpu.get_barrier_semaphore()
    for axis in range(3):
        for step in steps:
            pl.semaphore_signal(barrier, inc=1, device_id={"ctx": place.toward(axis, step)}, device_id_type=MESH)
    pl.semaphore_signal(barrier, inc=1, device_id={"dp": 1 - place.core}, device_id_type=MESH)
    for caller in callers:

        @pl.when(caller != place.me)
        def _():
            pl.semaphore_signal(barrier, inc=1, device_id={"ctx": caller}, device_id_type=MESH)

    count = 3 * len(steps) + 1
    for target in targets:
        count = count + jnp.where(target != place.me, 1, 0)
    pl.semaphore_wait(barrier, count)


def folded(half_block):
    return jnp.where(half_block < 64, half_block, 127 - half_block)


def swap_halves(v):
    return jnp.concatenate([v[:, HEAD // 2 :], v[:, : HEAD // 2]], axis=1)


def rms_forward(values, gain):
    inverse = lax.rsqrt(jnp.mean(values * values, axis=-1, keepdims=True) + EPS)
    return values * inverse * gain, inverse


def rms_backward(values, inverse, gain, grad):
    normal = values * inverse
    grad_gain = jnp.sum(grad * normal, axis=0, keepdims=True)
    scaled = grad * gain
    grad_in = inverse * (scaled - normal * jnp.mean(scaled * normal, axis=-1, keepdims=True))
    return grad_in, grad_gain


def start_kernel(
    x_in, trig_in, cot_in, gains_in, wq_in, wk_in, wv_in, wo_in, wg_in, wu_in, wd_in,
    xz, trig, cotz, gains, wq, wk, wv, wo, wg, wu, wd, h1_out, qpad, kv,
    zig_send, zig_recv, zig_local, dp_send, dp_recv, dp_local, ssem, rsem,
):
    place = Place()
    me = place.me
    targets = [folded(2 * me + k) for k in range(2)]
    owners = [me // 2, (127 - me) // 2]
    greet(place, (1, 3), owners, targets)
    slot = me // 32
    moved = ((x_in, xz), (trig_in, trig), (cot_in, cotz))

    def zig(k, n, src, dst):
        return src.at[pl.ds(HALF * k, HALF)], dst.at[pl.ds(pl.multiple_of(slot * HALF, HALF), HALF)]

    for n, (src, dst) in enumerate(moved):
        for k in range(2):
            a, b = zig(k, n, src, dst)

            @pl.when(targets[k] != me)
            def _():
                send(a, b, zig_send.at[n, k], zig_recv.at[n, slot], {"ctx": targets[k]})

            @pl.when(targets[k] == me)
            def _():
                pltpu.make_async_copy(a, b, zig_local.at[n]).start()

    other = {"dp": 1 - place.core}
    weights = ((gains_in, gains), (wq_in, wq), (wk_in, wk), (wv_in, wv), (wo_in, wo), (wg_in, wg), (wu_in, wu), (wd_in, wd))
    copies = []
    for n, (src, dst) in enumerate(weights):
        there = send(src, dst.at[place.core], dp_send.at[n], dp_recv.at[n], other)
        here = pltpu.make_async_copy(src, dst.at[place.core], dp_local.at[n])
        here.start()
        copies.append((there, here))

    def zig_wait(n):
        src, dst = moved[n]
        for side in range(2):
            ref = dst.at[pl.ds(side * HALF, HALF)]

            @pl.when(owners[side] != me)
            def _():
                arrived(ref, zig_send.at[n, 0], zig_recv.at[n, side], {"ctx": owners[side]})

            @pl.when(owners[side] == me)
            def _():
                pltpu.make_async_copy(ref, ref, zig_local.at[n]).wait()

    def dp_wait(n):
        dst = weights[n][1]
        copies[n][1].wait()
        arrived(dst.at[1 - place.core], dp_send.at[n], dp_recv.at[n], other)

    zig_wait(0)
    zig_wait(1)
    dp_wait(0)
    gain1 = jnp.concatenate([gains[0, 0:1, 0:288], gains[1, 0:1, 0:288]], axis=1)
    h1f, _ = rms_forward(xz[...].astype(F32), gain1)
    h1 = h1f.astype(BF16)
    h1_out[...] = h1
    for n in (1, 2, 3):
        dp_wait(n)

    def linear(w):
        return nn(h1[:, :288], w[0]) + nn(h1[:, 288:], w[1])

    cosines, sines = trig[:, 0:HEAD], trig[:, HEAD : 2 * HEAD]
    k_lin = linear(wk)
    v_lin = linear(wv)
    for h in range(KV_HEADS):
        cols = slice(h * HEAD, (h + 1) * HEAD)
        key = k_lin[:, cols]
        key = key * cosines + swap_halves(key) * sines
        kv[h, me // 16, lax.rem(me // 4, 4), lax.rem(me, 4)] = jnp.concatenate([key, v_lin[:, cols]], axis=1).astype(BF16)
    task = gather_task(place, kv, ROWS, ssem, rsem, lambda phase: None)
    next(task)
    q_lin = linear(wq)
    for h in range(HEADS):
        query = q_lin[:, h * HEAD : (h + 1) * HEAD]
        query = (query * cosines + swap_halves(query) * sines).astype(BF16)
        query = (query.astype(F32) * HEAD**-0.5).astype(BF16)
        query = jnp.concatenate([query, jnp.zeros((ROWS, HEAD), BF16)], axis=1)
        group = (h % GROUPS) * HALF
        qpad[h // GROUPS, group : group + HALF] = query[:HALF]
        qpad[h // GROUPS, 192 + group : 192 + group + HALF] = query[HALF:]
    run_together(task)
    zig_wait(2)
    for n in (4, 5, 6, 7):
        dp_wait(n)
    for there, _ in copies:
        there.wait_send()
    for n, (src, dst) in enumerate(moved):
        for k in range(2):

            @pl.when(targets[k] != me)
            def _():
                a, b = zig(k, n, src, dst)
                pltpu.make_async_remote_copy(
                    src_ref=a, dst_ref=b, send_sem=zig_send.at[n, k], recv_sem=zig_recv.at[n, slot],
                    device_id={"ctx": targets[k]}, device_id_type=MESH,
                ).wait_send()


def start_call(x, trig, cot, gains, weights):
    full = [shape((2, *w.shape), BF16) for w in weights]
    return pl.pallas_call(
        start_kernel,
        out_shape=(
            shape((ROWS, D), BF16), shape((ROWS, 128), F32), shape((ROWS, D), BF16), shape((2, 8, 384), F32),
            *full,
            shape((ROWS, D), BF16), shape((KV_HEADS, 384, 128), BF16), shape((KV_HEADS, 4, 4, 4, ROWS, 128), BF16),
        ),
        in_specs=anywhere(11),
        out_specs=(*vmem(7), *anywhere(4), *vmem(3)),
        scratch_shapes=[
            pltpu.SemaphoreType.DMA((3, 2)), pltpu.SemaphoreType.DMA((3, 2)), pltpu.SemaphoreType.DMA((3,)),
            pltpu.SemaphoreType.DMA((8,)), pltpu.SemaphoreType.DMA((8,)), pltpu.SemaphoreType.DMA((8,)),
            pltpu.SemaphoreType.DMA((3, 3, 6)), pltpu.SemaphoreType.DMA((3, 3, 6)),
        ],
        compiler_params=pltpu.CompilerParams(collective_id=0, has_side_effects=True, vmem_limit_bytes=VMEM_LIMIT),
        name="qkv_gather",
    )(x, trig, cot, gains, *weights)


def middle_kernel(
    xz, cotz, gains, qpad, kv, wo, wg, wu, wd, trig,
    result, e_out, dkv, dq_out, dx2_out,
    outs_t, lse, dopad, attn, dq_lin,
):
    me = lax.axis_index("ctx")
    mine = me // GROUP
    within = lax.rem(me, GROUP)
    key_row = lax.broadcasted_iota(jnp.int32, (KEYS, 384), 0)
    lane = lax.broadcasted_iota(jnp.int32, (KEYS, 384), 1)
    low_mask = key_row <= jnp.where(lane < 192, HALF * within + lax.rem(lane, HALF), KEYS)
    key_row = key_row[:, :192]
    lane = lane[:, :192]
    high_mask = lax.rem(key_row, HALF) - HALF * (key_row // HALF) <= lax.rem(lane, HALF) - HALF * within
    ones_lane = lax.broadcasted_iota(jnp.int32, (KEYS, 128), 1) < HEAD

    def keys_of(h, g, side):
        return kv[h, pl.ds(g * GROUP, GROUP), side * HALF : (side + 1) * HALF, :].reshape(KEYS, 128)

    def forward(h, _):
        def step(block, queries, mask, state):
            top, accum = state
            scores = nt(block, queries)
            if mask is not None:
                scores = jnp.where(mask, scores, MASKED)
            new_top = jnp.maximum(top, jnp.max(scores, axis=0, keepdims=True))
            weights = jnp.exp(scores - new_top).astype(BF16)
            values = jnp.where(ones_lane, jnp.ones_like(block), block)
            return new_top, accum * jnp.exp(top - new_top) + tn(values, weights)

        state = (jnp.full((1, 384), MASKED, F32), jnp.zeros((128, 384), F32))
        state = lax.fori_loop(0, mine, lambda g, s: step(keys_of(h, g, 0), qpad[h], None, s), state)
        top, accum = step(keys_of(h, mine, 0), qpad[h], low_mask, state)
        queries = qpad[h, 192:384]
        late = step(keys_of(h, mine, 1), queries, high_mask, (top[:, 192:], accum[:, 192:]))

        def both(g, s):
            s = step(keys_of(h, g, 0), queries, None, s)
            return step(keys_of(h, g, 1), queries, None, s)

        late = lax.fori_loop(mine + 1, 8, both, late)
        top = jnp.concatenate([top[:, :192], late[0]], axis=1)
        accum = jnp.concatenate([accum[:, :192], late[1]], axis=1)
        total = accum[0:1, :]
        outs = accum / total
        outs_t[h] = outs
        lse[h] = top + jnp.log(total)
        attn[h] = outs.T.astype(BF16)
        return 0

    lax.fori_loop(0, KV_HEADS, forward, 0)

    def by_token(ref, lanes):
        pieces = []
        for h in range(HEADS):
            group = (h % GROUPS) * HALF
            here = ref[h // GROUPS]
            pieces.append(jnp.concatenate([here[group : group + HALF, lanes], here[192 + group : 192 + group + HALF, lanes]], axis=0))
        return jnp.concatenate(pieces, axis=1)

    gain2 = jnp.concatenate([gains[0, 1:2, 0:288], gains[1, 1:2, 0:288]], axis=1)
    attn_low = by_token(attn, slice(64, 128))
    x = xz[...].astype(F32)
    x2 = x + nn(attn_low, wo[...])
    h2f, inverse2 = rms_forward(x2, gain2)
    h2 = h2f.astype(BF16)
    pad = jnp.zeros((ROWS, 64), BF16)
    dy_low = cotz[...]
    dy_pad = jnp.concatenate([dy_low, pad], axis=1)
    total = x2
    grad_h2 = jnp.zeros((ROWS, D), F32)

    def put(base, length, value, half, row):
        for tile in range(value.shape[1] // 128):
            at = base + tile * length + row
            e_out[half, at : at + value.shape[0], :] = value[:, tile * 128 : (tile + 1) * 128].astype(BF16)

    for t in range(3):
        cols = slice(512 * t, 512 * (t + 1))
        gate = nn(h2, wg[:, cols])
        up = nn(h2, wu[:, cols])
        sigma = jax.nn.sigmoid(gate)
        active = gate * sigma
        hidden = (active * up).astype(BF16)
        total = total + nn(hidden, wd[cols, :])
        grad_hidden = nt(dy_low, wd[cols, :])
        grad_gate = (grad_hidden * up * (sigma + active * (1.0 - sigma))).astype(BF16)
        grad_up = (grad_hidden * active).astype(BF16)
        grad_h2 = grad_h2 + nt(grad_gate, wg[:, cols]) + nt(grad_up, wu[:, cols])
        for base, value in ((E_GATE, tn(h2, grad_gate)), (E_UP, tn(h2, grad_up))):
            for half in range(2):
                put(base + 4 * t * 288, 288, value[288 * half : 288 * (half + 1)], half, 0)
        grad_down = tn(hidden, dy_pad)
        for s in range(2):
            index = 2 * t + s
            put(E_DOWN, 768, grad_down[256 * s : 256 * (s + 1)], index // 3, (index % 3) * 256)
    result[...] = total.astype(BF16)
    grad_norm2, grad_gain2 = rms_backward(x2, inverse2, gain2, grad_h2)
    grad_x2 = dy_low.astype(F32) + grad_norm2
    dx2_out[...] = grad_x2
    grad_attn = grad_x2.astype(BF16)
    grad_out = tn(attn_low, jnp.concatenate([grad_attn, pad], axis=1))
    for half in range(2):
        put(E_OUT, 288, grad_out[288 * half : 288 * (half + 1)], half, 0)
        line = jnp.concatenate([grad_gain2[:, 288 * half : 288 * (half + 1)], jnp.zeros((1, 96), F32)], axis=1)
        line = jnp.concatenate([line[:, 128 * k : 128 * (k + 1)] for k in range(3)] + [jnp.zeros((13, 128), F32)], axis=0)
        e_out[half, E_GAIN : E_GAIN + 16, :] = line.astype(BF16)
        e_out[half, E_GAIN + 16 : E_ROWS, :] = jnp.zeros((E_ROWS - E_GAIN - 16, 128), BF16)

    grad_o = nt(grad_attn, wo[...]).astype(BF16)
    for h in range(HEADS):
        piece = grad_o[:, h * HEAD : (h + 1) * HEAD]
        piece = jnp.concatenate([jnp.zeros((ROWS, HEAD), BF16), piece], axis=1)
        group = (h % GROUPS) * HALF
        dopad[h // GROUPS, group : group + HALF] = piece[:HALF]
        dopad[h // GROUPS, 192 + group : 192 + group + HALF] = piece[HALF:]

    def backward(h, _):
        delta = jnp.sum(dopad[h].astype(F32).T * outs_t[h], axis=0, keepdims=True)
        log_total = lse[h]

        def step(block, queries, grads, log_total, delta, mask, grad_q):
            scores = nt(block, queries)
            if mask is not None:
                scores = jnp.where(mask, scores, MASKED)
            probs = jnp.exp(scores - log_total)
            grad_scores = (probs * (nt(block, grads) - delta)).astype(BF16)
            part = nn(grad_scores, queries) + nn(probs.astype(BF16), grads)
            return grad_q + tn(block, grad_scores), part.astype(BF16)

        def save(g, side, part):
            dkv[h, pl.ds(g * GROUP, GROUP), side * HALF : (side + 1) * HALF, :] = part.reshape(GROUP, HALF, 128)

        def early(g, grad_q):
            grad_q, part = step(keys_of(h, g, 0), qpad[h], dopad[h], log_total, delta, None, grad_q)
            save(g, 0, part)
            save(g, 1, jnp.zeros((KEYS, 128), BF16))
            return grad_q

        grad_q = lax.fori_loop(0, mine, early, jnp.zeros((128, 384), F32))
        grad_q, part = step(keys_of(h, mine, 0), qpad[h], dopad[h], log_total, delta, low_mask, grad_q)
        save(mine, 0, part)
        queries, grads = qpad[h, 192:384], dopad[h, 192:384]
        log_late, delta_late = log_total[:, 192:], delta[:, 192:]
        late, part = step(keys_of(h, mine, 1), queries, grads, log_late, delta_late, high_mask, grad_q[:, 192:])
        save(mine, 1, part)

        def both(g, late):
            for side in range(2):
                late, part = step(keys_of(h, g, side), queries, grads, log_late, delta_late, None, late)
                save(g, side, part)
            return late

        late = lax.fori_loop(mine + 1, 8, both, late)
        dq_lin[h] = jnp.concatenate([grad_q[:, :192], late], axis=1).T
        return 0

    lax.fori_loop(0, KV_HEADS, backward, 0)
    cosines, sines = trig[:, 0:HEAD], trig[:, HEAD : 2 * HEAD]
    grad_q = by_token(dq_lin, slice(0, 64)) * HEAD**-0.5
    pieces = []
    for h in range(HEADS):
        piece = grad_q[:, h * HEAD : (h + 1) * HEAD]
        pieces.append(piece * cosines - swap_halves(piece) * sines)
    dq_out[...] = jnp.concatenate(pieces, axis=1).astype(BF16)


def middle_call(xz, cotz, gains, qpad, kv, wo, wg, wu, wd, trig):
    return pl.pallas_call(
        middle_kernel,
        out_shape=(
            shape((ROWS, D), BF16), shape((2, E_ROWS, 128), BF16), shape((KV_HEADS, 64, ROWS, 128), BF16),
            shape((ROWS, D), BF16), shape((ROWS, D), F32),
        ),
        in_specs=vmem(10),
        out_specs=tuple(vmem(5)),
        scratch_shapes=[
            pltpu.VMEM((KV_HEADS, 128, 384), F32), pltpu.VMEM((KV_HEADS, 1, 384), F32),
            pltpu.VMEM((KV_HEADS, 384, 128), BF16), pltpu.VMEM((KV_HEADS, 384, 128), BF16),
            pltpu.VMEM((KV_HEADS, 384, 128), F32),
        ],
        compiler_params=pltpu.CompilerParams(vmem_limit_bytes=VMEM_LIMIT),
        name="attention_and_ffn",
    )(xz, cotz, gains, qpad, kv, wo, wg, wu, wd, trig)


def end_kernel(
    dkv_in, e_in, dq, dx2, xz, h1, trig, gains, wq, wk, wv, result,
    e_sum, l_sum, out_result, out_grad,
    dkv, e_work, e_peer, l_full, l_peer, l_work, own, grad_z,
    kh0, kh1, kh2, kw0, kw1, kw2, eh0, eh1, eh2, ew0, ew1, ew2, ls0, ls1, ls2,
    ks, kr, es, er, gs, gr, ls, lr, ls2s, ls2r, dps, dpr, zs, zr, zl, local,
):
    place = Place()
    me, core = place.me, place.core
    owners = [me // 2, (127 - me) // 2]
    sources = [folded(2 * me + k) for k in range(2)]
    load = pltpu.make_async_copy(dkv_in, dkv, local.at[0])
    load.start()
    greet(place, (1, 2, 3), sources, owners)
    other = {"dp": 1 - core}
    e_copy = send(e_in.at[1 - core], e_peer, dps.at[0], dpr.at[0], other)
    e_load = pltpu.make_async_copy(e_in.at[core], e_work, local.at[1])
    e_load.start()

    def zig_send(n, src, dst):
        for side in range(2):
            half = (me, 127 - me)[side]
            k = lax.rem(half, 2)
            a = src.at[pl.ds(side * HALF, HALF)]
            b = dst.at[pl.ds(pl.multiple_of(k * HALF, HALF), HALF)]

            @pl.when(owners[side] != me)
            def _():
                send(a, b, zs.at[n, side], zr.at[n, k], {"ctx": owners[side]})

            @pl.when(owners[side] == me)
            def _():
                pltpu.make_async_copy(a, b, zl.at[n]).start()

    def zig_wait(n, src, dst):
        for k in range(2):
            ref = dst.at[pl.ds(k * HALF, HALF)]

            @pl.when(sources[k] != me)
            def _():
                arrived(ref, zs.at[n, 0], zr.at[n, k], {"ctx": sources[k]})

            @pl.when(sources[k] == me)
            def _():
                pltpu.make_async_copy(ref, ref, zl.at[n]).wait()

        for side in range(2):

            @pl.when(owners[side] != me)
            def _():
                a = src.at[pl.ds(side * HALF, HALF)]
                pltpu.make_async_remote_copy(
                    src_ref=a, dst_ref=a, send_sem=zs.at[n, side], recv_sem=zr.at[n, 0],
                    device_id={"ctx": owners[side]}, device_id_type=MESH,
                ).wait_send()

    zig_send(0, result, out_result)
    load.wait()

    def keep(part, index, total):
        own[part] = total

    def e_keep(part, index, total):
        e_sum[index] = total.astype(BF16)

    keys_task = scatter_task(place, dkv, (kh0, kh1, kh2), (kw0, kw1, kw2), ROWS, ks, kr, keep)

    def early():
        yield
        arrived(e_peer, dps.at[0], dpr.at[0], other)
        e_load.wait()
        for part in range(3):
            for z in range(4):
                add_into(e_work, (part, z), e_peer[part, z])
        yield from scatter_task(place, e_work, (eh0, eh1, eh2), (ew0, ew1, ew2), 64, es, er, e_keep)
        yield from gather_task(place, e_sum, 64, gs, gr, lambda phase: None)

    def late():
        yield from keys_task
        cosines, sines = trig[:, 0:HEAD], trig[:, HEAD : 2 * HEAD]
        gain1 = jnp.concatenate([gains[0, 0:1, 0:288], gains[1, 0:1, 0:288]], axis=1)
        keys, values = [], []
        for h in range(KV_HEADS):
            piece = own[h]
            grad_k = piece[:, :HEAD]
            keys.append(grad_k * cosines - swap_halves(grad_k) * sines)
            values.append(piece[:, HEAD:])
        dq_low = dq[...]
        dk_low = jnp.concatenate(keys, axis=1).astype(BF16)
        dv_low = jnp.concatenate(values, axis=1).astype(BF16)
        grads = jnp.concatenate([dq_low, dk_low, dv_low, jnp.zeros((ROWS, 64), BF16)], axis=1)
        weight_grads = tn(h1[...], grads)
        grad_h1 = nt(dq_low, wq[...]) + nt(dk_low, wk[...]) + nt(dv_low, wv[...])
        x = xz[...].astype(F32)
        inverse1 = lax.rsqrt(jnp.mean(x * x, axis=-1, keepdims=True) + EPS)
        grad_norm1, grad_gain1 = rms_backward(x, inverse1, gain1, grad_h1)
        for half in range(2):
            line = jnp.concatenate([grad_gain1[:, 288 * half : 288 * (half + 1)], jnp.zeros((1, 96), F32)], axis=1)
            line = jnp.concatenate([line[:, 128 * k : 128 * (k + 1)] for k in range(3)] + [jnp.zeros((13, 128), F32)], axis=0)
            for chunk in range(192):
                at = (half, chunk // 64, chunk // 16 % 4, chunk // 4 % 4, chunk % 4)
                tile, row = chunk // 18, 288 * half + 16 * (chunk % 18)
                if tile < 8:
                    l_full[at] = weight_grads[row : row + 16, 128 * tile : 128 * (tile + 1)].astype(BF16)
                else:
                    l_full[at] = line.astype(BF16) if chunk == 144 else jnp.zeros((16, 128), BF16)
        l_copy = send(l_full.at[1 - core], l_peer, dps.at[1], dpr.at[1], other)
        grad_z[...] = (dx2[...] + grad_norm1).astype(BF16)
        zig_send(1, grad_z, out_grad)
        yield
        arrived(l_peer, dps.at[1], dpr.at[1], other)
        for part in range(3):
            l_work[part] = (l_full[core, part].astype(F32) + l_peer[part].astype(F32)).astype(BF16)
        yield from small_sum_task(place, l_work, (ls0, ls1, ls2), l_sum, ls, lr, ls2s, ls2r)
        l_copy.wait_send()

    run_together(late(), early())
    e_copy.wait_send()
    zig_wait(0, result, out_result)
    zig_wait(1, grad_z, out_grad)


def end_call(dkv, e, dq, dx2, xz, h1, trig, gains, wq, wk, wv, result):
    def buffers(rows):
        dims = ((4, 4), (4,), ())
        halves = [pltpu.VMEM((3, 2, *d, rows // 2, 128), BF16) for d in dims]
        wholes = [pltpu.VMEM((3, 2, *d, rows, 128), BF16) for d in dims]
        return halves + wholes

    sem = pltpu.SemaphoreType.DMA
    return pl.pallas_call(
        end_kernel,
        out_shape=(
            shape((3, 4, 4, 4, 64, 128), BF16), shape((3, 4, 4, 4, 16, 128), BF16),
            shape((ROWS, D), BF16), shape((ROWS, D), BF16),
        ),
        in_specs=[*anywhere(2), *vmem(10)],
        out_specs=tuple(vmem(4)),
        scratch_shapes=[
            pltpu.VMEM((3, 4, 4, 4, ROWS, 128), BF16),
            pltpu.VMEM((3, 4, 4, 4, 64, 128), BF16), pltpu.VMEM((3, 4, 4, 4, 64, 128), BF16),
            pltpu.VMEM((2, 3, 4, 4, 4, 16, 128), BF16), pltpu.VMEM((3, 4, 4, 4, 16, 128), BF16), pltpu.VMEM((3, 4, 4, 4, 16, 128), BF16),
            pltpu.VMEM((3, ROWS, 128), F32), pltpu.VMEM((ROWS, D), BF16),
            *buffers(ROWS), *buffers(64),
            pltpu.VMEM((3, 3, 4, 4, 16, 128), BF16), pltpu.VMEM((3, 3, 4, 16, 128), BF16), pltpu.VMEM((3, 3, 16, 128), BF16),
            sem((3, 3, 6)), sem((3, 3, 6)), sem((3, 3, 6)), sem((3, 3, 6)), sem((3, 3, 6)), sem((3, 3, 6)),
            sem((3, 3, 3)), sem((3, 3, 3)), sem((3, 3, 3)), sem((3, 3, 3)),
            sem((2,)), sem((2,)), sem((2, 2)), sem((2, 2)), sem((2,)), sem((2,)),
        ],
        compiler_params=pltpu.CompilerParams(collective_id=1, has_side_effects=True, vmem_limit_bytes=VMEM_LIMIT),
        name="reduce_gradients",
    )(dkv, e, dq, dx2, xz, h1, trig, gains, wq, wk, wv, result)


def unpack_kernel(e, l, gain1, gq, gk, gv, go, gain2, gg, gu, gd):
    def take(ref, base, length, out):
        columns = out.shape[1]
        for tile in range(-(-columns // 128)):
            wide = min(128, columns - 128 * tile)
            at = base + tile * length
            out[:, 128 * tile : 128 * tile + wide] = ref[at : at + length, :wide].astype(F32)

    take(e, E_GATE, 288, gg)
    take(e, E_UP, 288, gu)
    take(e, E_DOWN, 768, gd)
    take(e, E_OUT, 288, go)
    gain2[...] = e[E_GAIN : E_GAIN + 16, :].astype(F32)
    gain1[...] = l[8 * 288 : 8 * 288 + 16, :].astype(F32)
    whole = jnp.concatenate([l[tile * 288 : (tile + 1) * 288, :] for tile in range(4, 8)], axis=1).astype(F32)
    take(l, 0, 288, gq)
    gk[...] = whole[:, 64:256]
    gv[...] = whole[:, 256:448]


def unpack_call(e, l):
    return pl.pallas_call(
        unpack_kernel,
        out_shape=(
            shape((16, 128), F32), shape((288, D), F32), shape((288, 192), F32), shape((288, 192), F32),
            shape((288, D), F32), shape((16, 128), F32), shape((288, FF), F32), shape((288, FF), F32), shape((768, D), F32),
        ),
        in_specs=vmem(2),
        out_specs=tuple(vmem(9)),
        compiler_params=pltpu.CompilerParams(vmem_limit_bytes=VMEM_LIMIT),
        name="unpack_gradients",
    )(e, l)


def body(
    layer_in, positions, norm_gain1, w_query, w_key, w_value, w_out, norm_gain2, w_gate, w_up, w_down, cotangent
):
    inv_freq = 10000.0 ** (-jnp.arange(HEAD // 2, dtype=F32) / (HEAD // 2))
    angles = positions[0].astype(F32)[:, None] * inv_freq[None, :]
    cosines, sines = jnp.cos(angles), jnp.sin(angles)
    trig = jnp.concatenate([cosines, cosines, -sines, sines], axis=1)
    gains = jnp.pad(jnp.stack([norm_gain1, norm_gain2]).astype(F32), ((0, 6), (0, 96)))
    xz, trig, cotz, gains, wq, wk, wv, wo, wg, wu, wd, h1, qpad, kv = start_call(
        layer_in[0], trig, cotangent[0], gains, (w_query, w_key, w_value, w_out, w_gate, w_up, w_down)
    )
    wq, wk, wv, wo, wg, wu, wd = (w.reshape(-1, w.shape[-1]) for w in (wq, wk, wv, wo, wg, wu, wd))
    result, e, dkv, dq, dx2 = middle_call(
        xz, cotz, gains, qpad, kv.reshape(KV_HEADS, 64, ROWS, 128), wo, wg, wu, wd, trig
    )
    e_sum, l_sum, result, grad = end_call(
        dkv.reshape(KV_HEADS, 4, 4, 4, ROWS, 128), e.reshape(2, 3, 4, 4, 4, 64, 128),
        dq, dx2, xz, h1, trig, gains, wq, wk, wv, result,
    )
    gain1, gq, gk, gv, go, gain2, gg, gu, gd = unpack_call(e_sum.reshape(-1, 128), l_sum.reshape(-1, 128))
    gain1, gain2 = (g[:3].reshape(-1)[:288] for g in (gain1, gain2))
    return (result[None], grad[None], gain1, gq, gk, gv, go, gain2, gg, gu, gd)


def solution(mesh):
    weight = P("dp", None)
    tokens = P("dp", "ctx", None)
    return jax.shard_map(
        body,
        mesh=mesh,
        in_specs=(tokens, P("dp", "ctx"), P("dp"), weight, weight, weight, weight, P("dp"), weight, weight, weight, tokens),
        out_specs=(tokens, tokens, P("dp"), weight, weight, weight, weight, P("dp"), weight, weight, weight),
        check_vma=False,
    )
```

```python
import jax
import jax.numpy as jnp
import numpy as np
from jax import lax
from jax.experimental import pallas as pl
from jax.experimental.pallas import tpu as pltpu
from jax.sharding import PartitionSpec as P

HEADS = 9
KV_HEADS = 3
GROUPS = HEADS // KV_HEADS
HEAD = 64
D = 576
FF = 1536
EPS = 1e-05
MASKED = -1e30
HALF = 64
GROUP = 8
KEYS = GROUP * HALF
ROWS = 2 * HALF
MESH = pl.DeviceIdType.MESH
F32 = jnp.float32
BF16 = jnp.bfloat16
VMEM_LIMIT = 60 * 1024 * 1024

E_GATE = 0
E_UP = 12 * 288
E_DOWN = 24 * 288
E_OUT = E_DOWN + 6 * 576
E_GAIN = E_OUT + 5 * 288
E_ROWS = 3 * 64 * 64


def vmem(n):
    return [pl.BlockSpec(memory_space=pltpu.VMEM)] * n


def anywhere(n):
    return [pl.BlockSpec(memory_space=pl.ANY)] * n


def shape(dims, dtype):
    return jax.ShapeDtypeStruct(dims, dtype)


def nn(a, b):
    return jnp.dot(a, b, preferred_element_type=F32)


def nt(a, b):
    return lax.dot_general(a, b, (((1,), (1,)), ((), ())), preferred_element_type=F32)


def tn(a, b):
    return lax.dot_general(a, b, (((0,), (0,)), ((), ())), preferred_element_type=F32)


def run_together(*tasks):
    tasks = list(tasks)
    while tasks:
        for task in list(tasks):
            try:
                next(task)
            except StopIteration:
                tasks.remove(task)


class Place:
    def __init__(self):
        self.core = lax.axis_index("dp")
        self.me = lax.axis_index("ctx")
        self.at = [lax.rem(self.me // 4**a, 4) for a in range(3)]
        self.coords = [[lax.rem(self.at[a] + step, 4) for step in range(4)] for a in range(3)]
        self.devices = [[self.me + (self.coords[a][step] - self.at[a]) * 4**a for step in range(4)] for a in range(3)]

    def toward(self, axis, step):
        return self.devices[axis][step]

    def coord(self, axis, step):
        return self.coords[axis][step]

    def region(self, part, phase, coord):
        index = [None, None, None]
        for k in range(3):
            axis = (part + k) % 3
            index[2 - axis] = pl.ds(0, 4) if k < phase else coord if k == phase else self.at[axis]
        return tuple(index)


def remote(src, dst, send_sem, recv_sem, device):
    return pltpu.make_async_remote_copy(
        src_ref=src, dst_ref=dst, send_sem=send_sem, recv_sem=recv_sem, device_id=device, device_id_type=MESH
    )


def send(src, dst, send_sem, recv_sem, device):
    copy = remote(src, dst, send_sem, recv_sem, device)
    copy.start()
    return copy


class Sends:
    def __init__(self):
        self.made = []

    def start(self, src, src_at, dst, dst_at, send_sem, recv_sem, at, device):
        def make():
            return remote(src.at[src_at], dst.at[dst_at], send_sem.at[at], recv_sem.at[at], device)

        make().start()
        self.made.append(make)

    def wait(self):
        for make in self.made:
            make().wait_send()


def arrived(dst, send_sem, recv_sem, device):
    pltpu.make_async_remote_copy(
        src_ref=dst, dst_ref=dst, send_sem=send_sem, recv_sem=recv_sem, device_id=device, device_id_type=MESH
    ).wait_recv()


def gather_task(place, buf, rows, ssem, rsem, done):
    first, second, whole = pl.ds(0, rows // 2), pl.ds(rows // 2, rows // 2), None
    sent = Sends()
    for phase in range(3):
        for part in range(3):
            axis = (part + phase) % 3
            plus, minus = {"ctx": place.toward(axis, 1)}, {"ctx": place.toward(axis, 3)}
            own = place.region(part, phase, place.at[axis])
            for k, (half, to) in enumerate(((first, plus), (second, minus), (second, plus), (first, minus))):
                index = (part, *own, half)
                sent.start(buf, index, buf, index, ssem, rsem, (part, phase, k), to)
        yield
        for part in range(3):
            axis = (part + phase) % 3
            plus, minus = {"ctx": place.toward(axis, 1)}, {"ctx": place.toward(axis, 3)}
            for k, (half, step, to) in enumerate(((first, 3, plus), (second, 1, minus))):
                index = (part, *place.region(part, phase, place.coord(axis, step)), half)
                arrived(buf.at[index], ssem.at[part, phase, k], rsem.at[part, phase, k], to)
                sent.start(buf, index, buf, index, ssem, rsem, (part, phase, 4 + k), to)
        yield
        for part in range(3):
            axis = (part + phase) % 3
            plus = {"ctx": place.toward(axis, 1)}
            for k, half, step in ((2, second, 3), (3, first, 1), (4, first, 2), (5, second, 2)):
                ref = buf.at[(part, *place.region(part, phase, place.coord(axis, step)), half)]
                arrived(ref, ssem.at[part, phase, k], rsem.at[part, phase, k], plus)
        done(phase)
    yield
    sent.wait()


def add_into(buf, index, other):
    buf[index] = (buf[index].astype(F32) + other.astype(F32)).astype(BF16)


def scatter_task(place, buf, halves, wholes, rows, ssem, rsem, finish):
    first, second = pl.ds(0, rows // 2), pl.ds(rows // 2, rows // 2)
    sent = Sends()
    for turn in range(3):
        phase = 2 - turn
        half_buf, whole_buf = halves[turn], wholes[turn]
        for part in range(3):
            axis = (part + phase) % 3
            plus, minus = {"ctx": place.toward(axis, 1)}, {"ctx": place.toward(axis, 3)}
            far = place.region(part, phase, place.coord(axis, 2))
            right = place.region(part, phase, place.coord(axis, 1))
            left = place.region(part, phase, place.coord(axis, 3))
            lead = (slice(None),) * phase
            for k, src, dst, to in (
                (0, (*far, first), (half_buf, (part, 0)), plus),
                (1, (*far, second), (half_buf, (part, 1)), minus),
                (2, (*right, second), (whole_buf, (part, 0, *lead, second)), plus),
                (3, (*left, first), (whole_buf, (part, 1, *lead, first)), minus),
            ):
                sent.start(buf, (part, *src), *dst, ssem, rsem, (part, turn, k), to)
        yield
        for part in range(3):
            axis = (part + phase) % 3
            plus, minus = {"ctx": place.toward(axis, 1)}, {"ctx": place.toward(axis, 3)}
            lead = (slice(None),) * phase
            for k, half, step, to in ((0, first, 1, plus), (1, second, 3, minus)):
                arrived(half_buf.at[part, k], ssem.at[part, turn, k], rsem.at[part, turn, k], to)
                index = (part, *place.region(part, phase, place.coord(axis, step)), half)
                add_into(buf, index, half_buf[part, k])
                sent.start(buf, index, whole_buf, (part, k, *lead, half), ssem, rsem, (part, turn, 4 + k), to)
        yield
        for part in range(3):
            axis = (part + phase) % 3
            plus = {"ctx": place.toward(axis, 1)}
            lead = (slice(None),) * phase
            for k, side, half in ((2, 0, second), (3, 1, first), (4, 0, first), (5, 1, second)):
                dst = whole_buf.at[(part, side, *lead, half)]
                arrived(dst, ssem.at[part, turn, k], rsem.at[part, turn, k], plus)
            index = (part, *place.region(part, phase, place.at[axis]))
            total = buf[index].astype(F32) + whole_buf[part, 0].astype(F32) + whole_buf[part, 1].astype(F32)
            if turn < 2:
                buf[index] = total.astype(BF16)
            else:
                finish(part, index, total)
    yield
    sent.wait()


def small_sum_task(place, buf, slots, out, ssem, rsem, ssem2, rsem2):
    sent = Sends()
    for turn in range(3):
        phase = 2 - turn
        for part in range(3):
            axis = (part + phase) % 3
            for k in range(3):
                index = (part, *place.region(part, phase, place.coord(axis, k + 1)))
                to = {"ctx": place.toward(axis, k + 1)}
                sent.start(buf, index, slots[turn], (part, k), ssem, rsem, (part, turn, k), to)
        yield
        for part in range(3):
            axis = (part + phase) % 3
            index = (part, *place.region(part, phase, place.at[axis]))
            total = buf[index].astype(F32)
            for k in range(3):
                to = {"ctx": place.toward(axis, k + 1)}
                arrived(slots[turn].at[part, k], ssem.at[part, turn, k], rsem.at[part, turn, k], to)
                total = total + slots[turn][part, k].astype(F32)
            if turn < 2:
                buf[index] = total.astype(BF16)
            else:
                out[index] = total.astype(BF16)
    for phase in range(3):
        for part in range(3):
            axis = (part + phase) % 3
            index = (part, *place.region(part, phase, place.at[axis]))
            for k in range(3):
                to = {"ctx": place.toward(axis, k + 1)}
                sent.start(out, index, out, index, ssem2, rsem2, (part, phase, k), to)
        yield
        for part in range(3):
            axis = (part + phase) % 3
            for k in range(3):
                to = {"ctx": place.toward(axis, k + 1)}
                ref = out.at[(part, *place.region(part, phase, place.coord(axis, 3 - k)))]
                arrived(ref, ssem2.at[part, phase, k], rsem2.at[part, phase, k], to)
    yield
    sent.wait()


def greet(place, partners):
    barrier = pltpu.get_barrier_semaphore()
    for axis in range(3):
        for step in (1, 2, 3):
            pl.semaphore_signal(barrier, inc=1, device_id={"ctx": place.toward(axis, step)}, device_id_type=MESH)
    pl.semaphore_signal(barrier, inc=1, device_id={"dp": 1 - place.core}, device_id_type=MESH)
    count = 10
    for partner in partners:

        @pl.when(partner != place.me)
        def _():
            pl.semaphore_signal(barrier, inc=1, device_id={"ctx": partner}, device_id_type=MESH)

        count = count + jnp.where(partner != place.me, 1, 0)
    pl.semaphore_wait(barrier, count)


def folded(half_block):
    return jnp.where(half_block < 64, half_block, 127 - half_block)


def swap_halves(v):
    return jnp.concatenate([v[:, HEAD // 2 :], v[:, : HEAD // 2]], axis=1)


def rms_forward(values, gain):
    inverse = lax.rsqrt(jnp.mean(values * values, axis=-1, keepdims=True) + EPS)
    return values * inverse * gain, inverse


def rms_backward(values, inverse, gain, grad):
    normal = values * inverse
    grad_gain = jnp.sum(grad * normal, axis=0, keepdims=True)
    scaled = grad * gain
    grad_in = inverse * (scaled - normal * jnp.mean(scaled * normal, axis=-1, keepdims=True))
    return grad_in, grad_gain


def layer_kernel(
    x_in, trig_in, cot_in, gain1_in, gain2_in, wq_in, wk_in, wv_in, wo_in, wg_in, wu_in, wd_in,
    e_sum, l_sum, out_result, out_grad,
    x_rows, cot_rows, g_rows, xz, trig, cotz, gains, wq, wk, wv, wo, wg, wu, wd, h1_kept, qpad, kv,
    outs_t, lse, dopad, attn, dq_early, dq_late, dq_rows, result, grad_x2_kept,
    dkv, e_all, e_peer, l_full, l_peer, l_work, own, grad_z,
    kh0, kh1, kh2, kw0, kw1, kw2, eh0, eh1, eh2, ew0, ew1, ew2, ls0, ls1, ls2,
    in_send, in_recv, in_local, dp_send, dp_recv, dp_local, as_, ar,
    ks, kr, es, er, gs, gr, ls, lr, ls2s, ls2r, dps, dpr, zs, zr, zl,
):
    place = Place()
    me, core = place.me, place.core
    every = range(KV_HEADS)

    x_rows[...] = x_in[...].T
    g_rows[...] = jnp.zeros((8, 384), F32)
    g_rows[0:1, 0:288] = gain1_in[...].astype(F32).reshape(1, 288)
    g_rows[1:2, 0:288] = gain2_in[...].astype(F32).reshape(1, 288)
    cot_rows[...] = cot_in[...].T
    targets = [folded(2 * me + k) for k in range(2)]
    owners = [me // 2, (127 - me) // 2]
    greet(place, owners + targets)
    slot = me // 32
    moved = ((x_rows, xz), (trig_in, trig), (cot_rows, cotz))

    def in_copy(n, k, here=False):
        src, dst = moved[n]
        a, b = src.at[pl.ds(HALF * k, HALF)], dst.at[pl.ds(pl.multiple_of(slot * HALF, HALF), HALF)]
        if here:
            return pltpu.make_async_copy(a, b, in_local.at[n])
        return remote(a, b, in_send.at[n, k], in_recv.at[n, slot], {"ctx": targets[k]})

    for n in range(3):
        for k in range(2):

            @pl.when(targets[k] != me)
            def _():
                in_copy(n, k).start()

            @pl.when(targets[k] == me)
            def _():
                in_copy(n, k, here=True).start()

    other = {"dp": 1 - core}
    weights = ((g_rows, gains), (wq_in, wq), (wk_in, wk), (wv_in, wv), (wo_in, wo), (wg_in, wg), (wu_in, wu), (wd_in, wd))
    copies = []
    for n, (src, dst) in enumerate(weights):
        there = send(src, dst.at[core], dp_send.at[n], dp_recv.at[n], other)
        here = pltpu.make_async_copy(src, dst.at[core], dp_local.at[n])
        here.start()
        copies.append((there, here))

    def in_wait(n):
        dst = moved[n][1]
        for side in range(2):
            ref = dst.at[pl.ds(side * HALF, HALF)]

            @pl.when(owners[side] != me)
            def _():
                arrived(ref, in_send.at[n, 0], in_recv.at[n, side], {"ctx": owners[side]})

            @pl.when(owners[side] == me)
            def _():
                pltpu.make_async_copy(ref, ref, in_local.at[n]).wait()

    def dp_wait(n):
        copies[n][1].wait()
        arrived(weights[n][1].at[1 - core], dp_send.at[n], dp_recv.at[n], other)

    in_wait(0)
    in_wait(1)
    dp_wait(0)
    gain1 = jnp.concatenate([gains[0, 0:1, 0:288], gains[1, 0:1, 0:288]], axis=1)
    gain2 = jnp.concatenate([gains[0, 1:2, 0:288], gains[1, 1:2, 0:288]], axis=1)
    x = xz[...].astype(F32)
    h1f, _ = rms_forward(x, gain1)
    h1 = h1f.astype(BF16)
    h1_kept[...] = h1
    for n in (1, 2, 3):
        dp_wait(n)

    def whole(ref):
        return ref[...].reshape(D, ref.shape[-1])

    cosines, sines = trig[:, 0:HEAD], trig[:, HEAD : 2 * HEAD]
    k_lin = nn(h1, whole(wk))
    v_lin = nn(h1, whole(wv))
    for h in every:
        cols = slice(h * HEAD, (h + 1) * HEAD)
        key = k_lin[:, cols]
        key = key * cosines + swap_halves(key) * sines
        kv[h, place.at[2], place.at[1], place.at[0]] = jnp.concatenate([key, v_lin[:, cols]], axis=1).astype(BF16)
    task = gather_task(place, kv, ROWS, as_, ar, lambda phase: None)
    next(task)
    q_lin = nn(h1, whole(wq))
    for h in range(HEADS):
        query = q_lin[:, h * HEAD : (h + 1) * HEAD]
        query = (query * cosines + swap_halves(query) * sines).astype(BF16)
        query = (query.astype(F32) * HEAD**-0.5).astype(BF16)
        query = jnp.concatenate([query, jnp.zeros((ROWS, HEAD), BF16)], axis=1)
        group = (h % GROUPS) * HALF
        qpad[h // GROUPS, group : group + HALF] = query[:HALF]
        qpad[h // GROUPS, 192 + group : 192 + group + HALF] = query[HALF:]
    run_together(task)
    in_wait(2)
    for n in (4, 5, 6, 7):
        dp_wait(n)

    mine = me // GROUP
    within = lax.rem(me, GROUP)
    key_row = lax.broadcasted_iota(jnp.int32, (KEYS, 384), 0)
    lane = lax.broadcasted_iota(jnp.int32, (KEYS, 384), 1)
    low_mask = key_row <= jnp.where(lane < 192, HALF * within + lax.rem(lane, HALF), KEYS)
    key_row = key_row[:, :192]
    lane = lane[:, :192]
    high_mask = lax.rem(key_row, HALF) - HALF * (key_row // HALF) <= lax.rem(lane, HALF) - HALF * within

    def keys_of(h, g, side):
        return kv[h, g // 2, pl.ds(2 * lax.rem(g, 2), 2), :, side * HALF : (side + 1) * HALF, :].reshape(KEYS, 128)

    def keys_both(h, g):
        return jnp.concatenate([keys_of(h, g, 0), keys_of(h, g, 1)], axis=0)

    def forward_step(block, queries, mask, state):
        top, accum = state
        scores = nt(block, queries)
        if mask is not None:
            scores = jnp.where(mask, scores, MASKED)
        new_top = jnp.maximum(top, jnp.max(scores, axis=0, keepdims=True))
        weights = jnp.exp(scores - new_top).astype(BF16)
        ones_lane = lax.broadcasted_iota(jnp.int32, block.shape, 1) < HEAD
        values = jnp.where(ones_lane, jnp.ones_like(block), block)
        return new_top, accum * jnp.exp(top - new_top) + tn(values, weights)

    late_rows = slice(192, 384)
    state = [(jnp.full((1, 384), MASKED, F32), jnp.zeros((128, 384), F32)) for h in every]
    state = lax.fori_loop(
        0, mine, lambda g, s: [forward_step(keys_of(h, g, 0), qpad[h], None, s[h]) for h in every], state
    )
    state = [forward_step(keys_of(h, mine, 0), qpad[h], low_mask, state[h]) for h in every]
    late = [
        forward_step(keys_of(h, mine, 1), qpad[h, late_rows], high_mask, (state[h][0][:, 192:], state[h][1][:, 192:]))
        for h in every
    ]
    late = lax.fori_loop(
        mine + 1, 8, lambda g, s: [forward_step(keys_both(h, g), qpad[h, late_rows], None, s[h]) for h in every], late
    )
    for h in every:
        top = jnp.concatenate([state[h][0][:, :192], late[h][0]], axis=1)
        accum = jnp.concatenate([state[h][1][:, :192], late[h][1]], axis=1)
        total = accum[0:1, :]
        outs = accum / total
        outs_t[h] = outs
        lse[h] = top + jnp.log(total)
        attn[h] = outs.T.astype(BF16)

    def by_token(ref, lanes):
        pieces = []
        for h in range(HEADS):
            group = (h % GROUPS) * HALF
            here = ref[h // GROUPS]
            pieces.append(jnp.concatenate([here[group : group + HALF, lanes], here[192 + group : 192 + group + HALF, lanes]], axis=0))
        return jnp.concatenate(pieces, axis=1)

    attn_low = by_token(attn, slice(64, 128))

    def put(base, length, value, half):
        for tile in range(value.shape[1] // 128):
            at, done = base + tile * length, 0
            while done < value.shape[0]:
                chunk, row = (at + done) // 64, (at + done) % 64
                size = min(64 - row, value.shape[0] - done)
                spot = (half, chunk // 64, chunk // 16 % 4, chunk // 4 % 4, chunk % 4, slice(row, row + size))
                e_all[spot] = value[done : done + size, tile * 128 : (tile + 1) * 128].astype(BF16)
                done += size

    def gain_line(grad, half):
        line = jnp.concatenate([grad[:, 288 * half : 288 * (half + 1)], jnp.zeros((1, 96), F32)], axis=1)
        return jnp.concatenate([line[:, 128 * k : 128 * (k + 1)] for k in range(3)] + [jnp.zeros((13, 128), F32)], axis=0)

    x2 = x + nn(attn_low, whole(wo))
    h2f, inverse2 = rms_forward(x2, gain2)
    h2 = h2f.astype(BF16)
    pad = jnp.zeros((ROWS, 64), BF16)
    dy_low = cotz[...]
    total = x2
    grad_h2 = jnp.zeros((ROWS, D), F32)
    for t in range(2):
        cols = slice(768 * t, 768 * (t + 1))
        wg_t, wu_t = wg[:, :, cols].reshape(D, 768), wu[:, :, cols].reshape(D, 768)
        gate = nn(h2, wg_t)
        up = nn(h2, wu_t)
        sigma = jax.nn.sigmoid(gate)
        active = gate * sigma
        hidden = (active * up).astype(BF16)
        total = total + nt(hidden, wd[t])
        grad_hidden = nn(dy_low, wd[t])
        grad_gate = (grad_hidden * up * (sigma + active * (1.0 - sigma))).astype(BF16)
        grad_up = (grad_hidden * active).astype(BF16)
        grad_h2 = grad_h2 + nt(grad_gate, wg_t) + nt(grad_up, wu_t)
        for base, value in ((E_GATE, tn(h2, grad_gate)), (E_UP, tn(h2, grad_up))):
            for half in range(2):
                put(base + 6 * t * 288, 288, value[288 * half : 288 * (half + 1)], half)
        put(E_DOWN, 576, tn(dy_low, hidden), t)
    result[...] = total.astype(BF16)
    grad_norm2, grad_gain2 = rms_backward(x2, inverse2, gain2, grad_h2)
    grad_x2 = dy_low.astype(F32) + grad_norm2
    grad_x2_kept[...] = grad_x2
    grad_attn = grad_x2.astype(BF16)
    grad_out = tn(attn_low, jnp.concatenate([grad_attn, pad], axis=1))
    for half in range(2):
        put(E_OUT, 288, grad_out[288 * half : 288 * (half + 1)], half)
        put(E_GAIN, 16, gain_line(grad_gain2, half), half)
        put(E_GAIN + 16, 0, jnp.zeros((E_ROWS - E_GAIN - 16, 128), F32), half)
    send(e_all.at[1 - core], e_peer, dps.at[0], dpr.at[0], other)

    def out_copy(n, side, here=False):
        src, dst = ((result, out_result), (grad_z, out_grad))[n]
        k = lax.rem((me, 127 - me)[side], 2)
        a = src.at[pl.ds(side * HALF, HALF)]
        b = dst.at[pl.ds(pl.multiple_of(k * HALF, HALF), HALF)]
        if here:
            return pltpu.make_async_copy(a, b, zl.at[n])
        return remote(a, b, zs.at[n, side], zr.at[n, k], {"ctx": owners[side]})

    def out_send(n):
        for side in range(2):

            @pl.when(owners[side] != me)
            def _():
                out_copy(n, side).start()

            @pl.when(owners[side] == me)
            def _():
                out_copy(n, side, here=True).start()

    def out_wait(n):
        dst = (out_result, out_grad)[n]
        for k in range(2):
            ref = dst.at[pl.ds(k * HALF, HALF)]

            @pl.when(targets[k] != me)
            def _():
                arrived(ref, zs.at[n, 0], zr.at[n, k], {"ctx": targets[k]})

            @pl.when(targets[k] == me)
            def _():
                pltpu.make_async_copy(ref, ref, zl.at[n]).wait()

        for side in range(2):

            @pl.when(owners[side] != me)
            def _():
                out_copy(n, side).wait_send()

    out_send(0)
    e_work = e_all.at[core]

    def early():
        arrived(e_peer, dps.at[0], dpr.at[0], other)
        remote(e_all.at[1 - core], e_peer, dps.at[0], dpr.at[0], other).wait_send()
        for part in range(3):
            for z in range(4):
                index = (core, part, z)
                e_all[index] = (e_all[index].astype(F32) + e_peer[part, z].astype(F32)).astype(BF16)

        def e_keep(part, index, total):
            e_sum[index] = total.astype(BF16)

        yield from scatter_task(place, e_work, (eh0, eh1, eh2), (ew0, ew1, ew2), 64, es, er, e_keep)
        yield from gather_task(place, e_sum, 64, gs, gr, lambda phase: None)

    early_task = early()

    grad_o = nt(grad_attn, whole(wo)).astype(BF16)
    for h in range(HEADS):
        piece = grad_o[:, h * HEAD : (h + 1) * HEAD]
        piece = jnp.concatenate([jnp.zeros((ROWS, HEAD), BF16), piece], axis=1)
        group = (h % GROUPS) * HALF
        dopad[h // GROUPS, group : group + HALF] = piece[:HALF]
        dopad[h // GROUPS, 192 + group : 192 + group + HALF] = piece[HALF:]

    deltas = [jnp.sum(dopad[h].astype(F32).T * outs_t[h], axis=0, keepdims=True) for h in every]
    logs = [lse[h] for h in every]

    def backward_step(block, queries, grads, log_total, delta, mask, grad_q):
        scores = nt(block, queries)
        if mask is not None:
            scores = jnp.where(mask, scores, MASKED)
        probs = jnp.exp(scores - log_total)
        grad_scores = (probs * (nt(block, grads) - delta)).astype(BF16)
        part = nn(grad_scores, queries) + nn(probs.astype(BF16), grads)
        return grad_q + tn(block, grad_scores), part.astype(BF16)

    def save(h, g, side, part):
        spot = (h, g // 2, pl.ds(2 * lax.rem(g, 2), 2), slice(None), slice(side * HALF, (side + 1) * HALF))
        dkv[spot] = part.reshape(2, 4, HALF, 128)

    dq_early[...] = jnp.zeros_like(dq_early)
    dq_late[...] = jnp.zeros_like(dq_late)

    def early_keys(g, mask):
        for h in every:
            dq_early[h], part = backward_step(
                keys_of(h, g, 0), qpad[h], dopad[h], logs[h], deltas[h], mask, dq_early[h]
            )
            save(h, g, 0, part)

    def late_keys(block_of, g, mask):
        parts = []
        for h in every:
            dq_late[h], part = backward_step(
                block_of(h, g), qpad[h, late_rows], dopad[h, late_rows], logs[h][:, 192:], deltas[h][:, 192:],
                mask, dq_late[h],
            )
            parts.append(part)
        return parts

    def backward(g, _):
        for k in range(8):

            @pl.when(g == k)
            def _():
                next(early_task)

        @pl.when(g < mine)
        def _():
            early_keys(g, None)
            for h in every:
                save(h, g, 1, jnp.zeros((KEYS, 128), BF16))

        @pl.when(g == mine)
        def _():
            early_keys(g, low_mask)
            for h, part in enumerate(late_keys(lambda h, g: keys_of(h, g, 1), g, high_mask)):
                save(h, g, 1, part)

        @pl.when(g > mine)
        def _():
            for h, part in enumerate(late_keys(keys_both, g, None)):
                save(h, g, 0, part[:KEYS])
                save(h, g, 1, part[KEYS:])

        return 0

    lax.fori_loop(0, 8, backward, 0)

    def keep(part, index, total):
        own[part] = total

    keys_task = scatter_task(place, dkv, (kh0, kh1, kh2), (kw0, kw1, kw2), ROWS, ks, kr, keep)

    def late_part():
        next(keys_task)
        for h in every:
            dq_rows[h] = jnp.concatenate([dq_early[h][:, :192], dq_early[h][:, 192:] + dq_late[h]], axis=1).T
        grad_q = by_token(dq_rows, slice(0, 64)) * HEAD**-0.5
        pieces = []
        for h in range(HEADS):
            piece = grad_q[:, h * HEAD : (h + 1) * HEAD]
            pieces.append(piece * cosines - swap_halves(piece) * sines)
        dq_low = jnp.concatenate(pieces, axis=1).astype(BF16)
        grad_h1 = nt(dq_low, whole(wq))
        yield from keys_task
        keys, values = [], []
        for h in every:
            piece = own[h]
            grad_k = piece[:, :HEAD]
            keys.append(grad_k * cosines - swap_halves(grad_k) * sines)
            values.append(piece[:, HEAD:])
        dk_low = jnp.concatenate(keys, axis=1).astype(BF16)
        dv_low = jnp.concatenate(values, axis=1).astype(BF16)
        grads = jnp.concatenate([dq_low, dk_low, dv_low, jnp.zeros((ROWS, 64), BF16)], axis=1)
        weight_grads = tn(h1_kept[...], grads)
        grad_h1 = grad_h1 + nt(dk_low, whole(wk)) + nt(dv_low, whole(wv))
        x = xz[...].astype(F32)
        inverse1 = lax.rsqrt(jnp.mean(x * x, axis=-1, keepdims=True) + EPS)
        grad_norm1, grad_gain1 = rms_backward(x, inverse1, gain1, grad_h1)
        for half in range(2):
            line = gain_line(grad_gain1, half).astype(BF16)
            for chunk in range(192):
                at = (half, chunk // 64, chunk // 16 % 4, chunk // 4 % 4, chunk % 4)
                tile, row = chunk // 18, 288 * half + 16 * (chunk % 18)
                if tile < 8:
                    l_full[at] = weight_grads[row : row + 16, 128 * tile : 128 * (tile + 1)].astype(BF16)
                else:
                    l_full[at] = line if chunk == 144 else jnp.zeros((16, 128), BF16)
        l_copy = send(l_full.at[1 - core], l_peer, dps.at[1], dpr.at[1], other)
        grad_z[...] = (grad_x2_kept[...] + grad_norm1).astype(BF16)
        out_send(1)
        yield
        arrived(l_peer, dps.at[1], dpr.at[1], other)
        for part in range(3):
            l_work[part] = (l_full[core, part].astype(F32) + l_peer[part].astype(F32)).astype(BF16)
        yield from small_sum_task(place, l_work, (ls0, ls1, ls2), l_sum, ls, lr, ls2s, ls2r)
        l_copy.wait_send()

    run_together(late_part(), early_task)
    out_wait(0)
    out_wait(1)
    for there, _ in copies:
        there.wait_send()
    for n in range(3):
        for k in range(2):

            @pl.when(targets[k] != me)
            def _():
                in_copy(n, k).wait_send()


def layer_call(x, trig, cot, gain1, gain2, weights):
    def buffers(rows):
        dims = ((4, 4), (4,), ())
        halves = [pltpu.VMEM((3, 2, *d, rows // 2, 128), BF16) for d in dims]
        wholes = [pltpu.VMEM((3, 2, *d, rows, 128), BF16) for d in dims]
        return halves + wholes

    sem = pltpu.SemaphoreType.DMA
    v = pltpu.VMEM
    return pl.pallas_call(
        layer_kernel,
        out_shape=(
            shape((3, 4, 4, 4, 64, 128), BF16), shape((3, 4, 4, 4, 16, 128), BF16),
            shape((ROWS, D), BF16), shape((ROWS, D), BF16),
        ),
        in_specs=(*vmem(5), *anywhere(7)),
        out_specs=tuple(vmem(4)),
        scratch_shapes=[
            v((ROWS, D), BF16), v((ROWS, D), BF16), v((8, 384), F32),
            v((ROWS, D), BF16), v((ROWS, 128), F32), v((ROWS, D), BF16), v((2, 8, 384), F32),
            *[v((2, *w.shape), BF16) for w in weights],
            v((ROWS, D), BF16), v((KV_HEADS, 384, 128), BF16), v((KV_HEADS, 4, 4, 4, ROWS, 128), BF16),
            v((KV_HEADS, 128, 384), F32), v((KV_HEADS, 1, 384), F32), v((KV_HEADS, 384, 128), BF16),
            v((KV_HEADS, 384, 128), BF16), v((KV_HEADS, 128, 384), F32), v((KV_HEADS, 128, 192), F32),
            v((KV_HEADS, 384, 128), F32), v((ROWS, D), BF16), v((ROWS, D), F32),
            v((3, 4, 4, 4, ROWS, 128), BF16), v((2, 3, 4, 4, 4, 64, 128), BF16), v((3, 4, 4, 4, 64, 128), BF16),
            v((2, 3, 4, 4, 4, 16, 128), BF16), v((3, 4, 4, 4, 16, 128), BF16), v((3, 4, 4, 4, 16, 128), BF16),
            v((3, ROWS, 128), F32), v((ROWS, D), BF16),
            *buffers(ROWS), *buffers(64),
            v((3, 3, 4, 4, 16, 128), BF16), v((3, 3, 4, 16, 128), BF16), v((3, 3, 16, 128), BF16),
            sem((3, 2)), sem((3, 2)), sem((3,)), sem((8,)), sem((8,)), sem((8,)), sem((3, 3, 6)), sem((3, 3, 6)),
            sem((3, 3, 6)), sem((3, 3, 6)), sem((3, 3, 6)), sem((3, 3, 6)), sem((3, 3, 6)), sem((3, 3, 6)),
            sem((3, 3, 3)), sem((3, 3, 3)), sem((3, 3, 3)), sem((3, 3, 3)),
            sem((2,)), sem((2,)), sem((2, 2)), sem((2, 2)), sem((2,)),
        ],
        compiler_params=pltpu.CompilerParams(collective_id=0, has_side_effects=True, vmem_limit_bytes=VMEM_LIMIT),
        name="decoder_layer",
    )(x, trig, cot, gain1, gain2, *weights)


def unpack_kernel(e, l, result, grad, result_t, grad_t, gain1, gq, gk, gv, go, gain2, gg, gu, gd):
    def take(ref, base, length, out):
        columns = out.shape[1]
        for tile in range(-(-columns // 128)):
            wide = min(128, columns - 128 * tile)
            at = base + tile * length
            out[:, 128 * tile : 128 * tile + wide] = ref[at : at + length, :wide].astype(F32)

    take(e, E_GATE, 288, gg)
    take(e, E_UP, 288, gu)
    take(e, E_DOWN, 576, gd)
    result_t[...] = result[...].T
    grad_t[...] = grad[...].T
    take(e, E_OUT, 288, go)
    gain2[...] = e[E_GAIN : E_GAIN + 16, :].astype(F32)
    gain1[...] = l[8 * 288 : 8 * 288 + 16, :].astype(F32)
    whole = jnp.concatenate([l[tile * 288 : (tile + 1) * 288, :] for tile in range(4, 8)], axis=1).astype(F32)
    take(l, 0, 288, gq)
    gk[...] = whole[:, 64:256]
    gv[...] = whole[:, 256:448]


def unpack_call(e, l, result, grad):
    return pl.pallas_call(
        unpack_kernel,
        out_shape=(
            shape((D, ROWS), BF16), shape((D, ROWS), BF16),
            shape((16, 128), F32), shape((288, D), F32), shape((288, 192), F32), shape((288, 192), F32),
            shape((288, D), F32), shape((16, 128), F32), shape((288, FF), F32), shape((288, FF), F32), shape((D, 768), F32),
        ),
        in_specs=vmem(4),
        out_specs=tuple(vmem(11)),
        compiler_params=pltpu.CompilerParams(vmem_limit_bytes=VMEM_LIMIT),
        name="unpack_gradients",
    )(e, l, result, grad)


def body(
    layer_in, positions, norm_gain1, w_query, w_key, w_value, w_out, norm_gain2, w_gate, w_up, w_down, cotangent
):
    inv_freq = np.tile(10000.0 ** (-np.arange(HEAD // 2) / (HEAD // 2)), 4).astype(np.float32)
    angles = positions[0].astype(F32)[:, None] * inv_freq[None, :]
    lane = lax.broadcasted_iota(jnp.int32, (ROWS, 128), 1)
    sines = jnp.sin(angles)
    trig = jnp.where(lane < 64, jnp.cos(angles), jnp.where(lane < 96, -sines, sines))
    e_sum, l_sum, result, grad = layer_call(
        layer_in[0].T, trig, cotangent[0].T, norm_gain1, norm_gain2,
        (w_query, w_key, w_value, w_out, w_gate, w_up, w_down.T),
    )
    result, grad, gain1, gq, gk, gv, go, gain2, gg, gu, gd = unpack_call(
        e_sum.reshape(-1, 128), l_sum.reshape(-1, 128), result, grad
    )
    gain1, gain2 = (g[:3].reshape(-1)[:288] for g in (gain1, gain2))
    return (result.T[None], grad.T[None], gain1, gq, gk, gv, go, gain2, gg, gu, gd.T)


def solution(mesh):
    weight = P("dp", None)
    tokens = P("dp", "ctx", None)
    return jax.shard_map(
        body,
        mesh=mesh,
        in_specs=(tokens, P("dp", "ctx"), P("dp"), weight, weight, weight, weight, P("dp"), weight, weight, weight, tokens),
        out_specs=(tokens, tokens, P("dp"), weight, weight, weight, weight, P("dp"), weight, weight, weight),
        check_vma=False,
    )
```

```python
import jax
import jax.numpy as jnp
import numpy as np
from jax import lax
from jax.experimental import pallas as pl
from jax.experimental.pallas import tpu as pltpu
from jax.sharding import PartitionSpec as P

HEADS = 9
KV_HEADS = 3
GROUPS = HEADS // KV_HEADS
HEAD = 64
D = 576
FF = 1536
EPS = 1e-05
MASKED = -1e30
HALF = 64
ROWS = 2 * HALF
MESH = pl.DeviceIdType.MESH
F32 = jnp.float32
BF16 = jnp.bfloat16
VMEM_LIMIT = 60 * 1024 * 1024

E_GATE = 0
E_UP = 12 * 288
E_DOWN = 24 * 288
E_OUT = E_DOWN + 6 * 576
E_GAIN = E_OUT + 5 * 288
E_ROWS = 3 * 64 * 64


def vmem(n):
    return [pl.BlockSpec(memory_space=pltpu.VMEM)] * n


def anywhere(n):
    return [pl.BlockSpec(memory_space=pl.ANY)] * n


def shape(dims, dtype):
    return jax.ShapeDtypeStruct(dims, dtype)


def nn(a, b):
    return jnp.dot(a, b, preferred_element_type=F32)


def nt(a, b):
    return lax.dot_general(a, b, (((1,), (1,)), ((), ())), preferred_element_type=F32)


def tn(a, b):
    return lax.dot_general(a, b, (((0,), (0,)), ((), ())), preferred_element_type=F32)


def run_together(*tasks):
    tasks = list(tasks)
    while tasks:
        for task in list(tasks):
            try:
                next(task)
            except StopIteration:
                tasks.remove(task)


class Place:
    def __init__(self):
        self.core = lax.axis_index("dp")
        self.me = lax.axis_index("ctx")
        self.at = [lax.rem(self.me // 4**a, 4) for a in range(3)]
        self.coords = [[lax.rem(self.at[a] + step, 4) for step in range(4)] for a in range(3)]
        self.plane = [(dy, dx) for dy in range(4) for dx in range(4) if dy or dx]
        self.devices = [[self.me + (self.coords[a][step] - self.at[a]) * 4**a for step in range(4)] for a in range(3)]

    def toward(self, axis, step):
        return self.devices[axis][step]

    def in_plane(self, dy, dx):
        return self.devices[1][dy] + self.devices[0][dx] - self.me

    def coord(self, axis, step):
        return self.coords[axis][step]

    def region(self, part, phase, coord):
        index = [None, None, None]
        for k in range(3):
            axis = (part + k) % 3
            index[2 - axis] = pl.ds(0, 4) if k < phase else coord if k == phase else self.at[axis]
        return tuple(index)


def remote(src, dst, send_sem, recv_sem, device):
    return pltpu.make_async_remote_copy(
        src_ref=src, dst_ref=dst, send_sem=send_sem, recv_sem=recv_sem, device_id=device, device_id_type=MESH
    )


def send(src, dst, send_sem, recv_sem, device):
    copy = remote(src, dst, send_sem, recv_sem, device)
    copy.start()
    return copy


class Sends:
    def __init__(self):
        self.made = []

    def start(self, src, src_at, dst, dst_at, send_sem, recv_sem, at, device):
        def make():
            return remote(src.at[src_at], dst.at[dst_at], send_sem.at[at], recv_sem.at[at], device)

        make().start()
        self.made.append(make)

    def wait(self):
        for make in self.made:
            make().wait_send()


def arrived(dst, send_sem, recv_sem, device):
    pltpu.make_async_remote_copy(
        src_ref=dst, dst_ref=dst, send_sem=send_sem, recv_sem=recv_sem, device_id=device, device_id_type=MESH
    ).wait_recv()


def gather_task(place, buf, row, rows, ssem, rsem):
    first, second = pl.ds(row, rows // 2), pl.ds(row + rows // 2, rows // 2)
    sent = Sends()
    for phase in range(3):
        for part in range(3):
            axis = (part + phase) % 3
            plus, minus = {"ctx": place.toward(axis, 1)}, {"ctx": place.toward(axis, 3)}
            own = place.region(part, phase, place.at[axis])
            for k, (half, to) in enumerate(((first, plus), (second, minus), (second, plus), (first, minus))):
                index = (part, *own, half)
                sent.start(buf, index, buf, index, ssem, rsem, (part, phase, k), to)
        yield
        for part in range(3):
            axis = (part + phase) % 3
            plus, minus = {"ctx": place.toward(axis, 1)}, {"ctx": place.toward(axis, 3)}
            for k, (half, step, to) in enumerate(((first, 3, plus), (second, 1, minus))):
                index = (part, *place.region(part, phase, place.coord(axis, step)), half)
                arrived(buf.at[index], ssem.at[part, phase, k], rsem.at[part, phase, k], to)
                sent.start(buf, index, buf, index, ssem, rsem, (part, phase, 4 + k), to)
        yield
        for part in range(3):
            axis = (part + phase) % 3
            plus = {"ctx": place.toward(axis, 1)}
            for k, half, step in ((2, second, 3), (3, first, 1)):
                ref = buf.at[(part, *place.region(part, phase, place.coord(axis, step)), half)]
                arrived(ref, ssem.at[part, phase, k], rsem.at[part, phase, k], plus)
        if phase == 2:
            yield
        for part in range(3):
            axis = (part + phase) % 3
            plus = {"ctx": place.toward(axis, 1)}
            for k, half, step in ((4, first, 2), (5, second, 2)):
                ref = buf.at[(part, *place.region(part, phase, place.coord(axis, step)), half)]
                arrived(ref, ssem.at[part, phase, k], rsem.at[part, phase, k], plus)
    yield
    sent.wait()


def add_into(buf, index, other):
    buf[index] = (buf[index].astype(F32) + other.astype(F32)).astype(BF16)


def scatter_task(place, buf, halves, wholes, rows, ssem, rsem, finish, stepwise=False):
    first, second = pl.ds(0, rows // 2), pl.ds(rows // 2, rows // 2)
    sent = Sends()
    for turn in range(3):
        phase = 2 - turn
        half_buf, whole_buf = halves[turn], wholes[turn]
        for near in range(2):
            for part in range(3):
                axis = (part + phase) % 3
                plus, minus = {"ctx": place.toward(axis, 1)}, {"ctx": place.toward(axis, 3)}
                far = place.region(part, phase, place.coord(axis, 2))
                right = place.region(part, phase, place.coord(axis, 1))
                left = place.region(part, phase, place.coord(axis, 3))
                lead = (slice(None),) * phase
                for k, src, dst, to in (
                    (0, (*far, first), (half_buf, (part, 0)), plus),
                    (1, (*far, second), (half_buf, (part, 1)), minus),
                    (2, (*right, second), (whole_buf, (part, 0, *lead, second)), plus),
                    (3, (*left, first), (whole_buf, (part, 1, *lead, first)), minus),
                )[2 * near : 2 * near + 2]:
                    sent.start(buf, (part, *src), *dst, ssem, rsem, (part, turn, k), to)
            if stepwise and turn == 0 and near == 0:
                yield
        yield
        for part in range(3):
            axis = (part + phase) % 3
            plus, minus = {"ctx": place.toward(axis, 1)}, {"ctx": place.toward(axis, 3)}
            lead = (slice(None),) * phase
            for k, half, step, to in ((0, first, 1, plus), (1, second, 3, minus)):
                arrived(half_buf.at[part, k], ssem.at[part, turn, k], rsem.at[part, turn, k], to)
                index = (part, *place.region(part, phase, place.coord(axis, step)), half)
                add_into(buf, index, half_buf[part, k])
                sent.start(buf, index, whole_buf, (part, k, *lead, half), ssem, rsem, (part, turn, 4 + k), to)
        yield
        for part in range(3):
            axis = (part + phase) % 3
            plus = {"ctx": place.toward(axis, 1)}
            lead = (slice(None),) * phase
            for k, side, half in ((2, 0, second), (3, 1, first), (4, 0, first), (5, 1, second)):
                dst = whole_buf.at[(part, side, *lead, half)]
                arrived(dst, ssem.at[part, turn, k], rsem.at[part, turn, k], plus)
            index = (part, *place.region(part, phase, place.at[axis]))
            total = buf[index].astype(F32) + whole_buf[part, 0].astype(F32) + whole_buf[part, 1].astype(F32)
            if turn < 2:
                buf[index] = total.astype(BF16)
            else:
                finish(part, index, total)
    yield
    sent.wait()


def plane_sum_task(place, buf, slots, layers, out, sems):
    sent = Sends()
    here = (place.at[1], place.at[0])
    there, back, peers = [], [], []
    for dy, dx in place.plane:
        there.append((place.coord(1, dy), place.coord(0, dx)))
        back.append((place.coord(1, (4 - dy) % 4), place.coord(0, (4 - dx) % 4)))
        peers.append({"ctx": place.in_plane(dy, dx)})
    for k, to in enumerate(peers):
        sent.start(buf, there[k], slots, k, sems[0], sems[1], k, to)
    yield
    total = buf[here].astype(F32)
    for k, to in enumerate(peers):
        arrived(slots.at[k], sems[0].at[k], sems[1].at[k], to)
        total = total + slots[k].astype(F32)
    layers[place.at[2]] = total.astype(BF16)
    for k in range(3):
        to = {"ctx": place.toward(2, k + 1)}
        sent.start(layers, place.at[2], layers, place.at[2], sems[2], sems[3], k, to)
    yield
    for k in range(3):
        to = {"ctx": place.toward(2, k + 1)}
        arrived(layers.at[place.coord(2, 3 - k)], sems[2].at[k], sems[3].at[k], to)
    total = layers[0].astype(F32)
    for z in range(1, 4):
        total = total + layers[z].astype(F32)
    out[here] = total.astype(BF16)
    for k, to in enumerate(peers):
        sent.start(out, here, out, here, sems[4], sems[5], k, to)
    yield
    for k, to in enumerate(peers):
        arrived(out.at[back[k]], sems[4].at[k], sems[5].at[k], to)
    yield
    sent.wait()


def greet(place, partners):
    barrier = pltpu.get_barrier_semaphore()
    for step in (1, 2, 3):
        pl.semaphore_signal(barrier, inc=1, device_id={"ctx": place.toward(2, step)}, device_id_type=MESH)
    for dy, dx in place.plane:
        pl.semaphore_signal(barrier, inc=1, device_id={"ctx": place.in_plane(dy, dx)}, device_id_type=MESH)
    pl.semaphore_signal(barrier, inc=1, device_id={"dp": 1 - place.core}, device_id_type=MESH)
    count = 19
    for partner in partners:

        @pl.when(partner != place.me)
        def _():
            pl.semaphore_signal(barrier, inc=1, device_id={"ctx": partner}, device_id_type=MESH)

        count = count + jnp.where(partner != place.me, 1, 0)
    pl.semaphore_wait(barrier, count)


def folded(half_block):
    return jnp.where(half_block < 64, half_block, 127 - half_block)


def swap_halves(v):
    return jnp.concatenate([v[:, HEAD // 2 :], v[:, : HEAD // 2]], axis=1)


def rms_forward(values, gain):
    inverse = lax.rsqrt(jnp.mean(values * values, axis=-1, keepdims=True) + EPS)
    return values * inverse * gain, inverse


def rms_backward(values, inverse, gain, grad):
    normal = values * inverse
    grad_gain = jnp.sum(grad * normal, axis=0, keepdims=True)
    scaled = grad * gain
    grad_in = inverse * (scaled - normal * jnp.mean(scaled * normal, axis=-1, keepdims=True))
    return grad_in, grad_gain


def layer_kernel(
    x_in, trig_in, cot_in, gain1_in, gain2_in, wq_in, wk_in, wv_in, wo_in, wg_in, wu_in, wd_in,
    e_sum, m_sum, l_sum, out_result, out_grad,
    x_rows, cot_rows, g_rows, xz, trig, cotz, gains, wq, wk, wv, wo, wg, wu, wd, h1_kept, qpad, kv,
    top_ab, acc_ab, top_b, acc_b, outs_t, lse, dopad, attn, dq_early, dq_late, dq_rows, result, grad_x2_kept,
    dkv, e_all, e_peer, m_full, m_peer, m_work, m_slots, m_layers, l_full, l_peer, l_work, l_slots, l_layers, own, grad_z,
    kh0, kh1, kh2, kw0, kw1, kw2, eh0, eh1, eh2, ew0, ew1, ew2,
    in_send, in_recv, in_local, dp_send, dp_recv, dp_local, as_, ar,
    ks, kr, es, er, gs, gr, m0, m1, m2, m3, m4, m5, l0, l1, l2, l3, l4, l5, dps, dpr, zs, zr, zl,
):
    place = Place()
    me, core = place.me, place.core
    every = range(KV_HEADS)

    x_rows[...] = x_in[...].T
    g_rows[...] = jnp.zeros((8, 384), F32)
    g_rows[0:1, 0:288] = gain1_in[...].astype(F32).reshape(1, 288)
    g_rows[1:2, 0:288] = gain2_in[...].astype(F32).reshape(1, 288)
    cot_rows[...] = cot_in[...].T
    targets = [folded(2 * me + k) for k in range(2)]
    owners = [me // 2, (127 - me) // 2]
    greet(place, owners + targets)
    slot = me // 32
    moved = ((x_rows, xz), (trig_in, trig), (cot_rows, cotz))

    def in_copy(n, k, here=False):
        src, dst = moved[n]
        a, b = src.at[pl.ds(HALF * k, HALF)], dst.at[pl.ds(pl.multiple_of(slot * HALF, HALF), HALF)]
        if here:
            return pltpu.make_async_copy(a, b, in_local.at[n])
        return remote(a, b, in_send.at[n, k], in_recv.at[n, slot], {"ctx": targets[k]})

    for n in range(3):
        for k in range(2):

            @pl.when(targets[k] != me)
            def _():
                in_copy(n, k).start()

            @pl.when(targets[k] == me)
            def _():
                in_copy(n, k, here=True).start()

    other = {"dp": 1 - core}
    weights = ((g_rows, gains), (wk_in, wk), (wv_in, wv), (wq_in, wq), (wo_in, wo), (wg_in, wg), (wu_in, wu), (wd_in, wd))
    copies = []
    for n, (src, dst) in enumerate(weights):
        there = send(src, dst.at[core], dp_send.at[n], dp_recv.at[n], other)
        here = pltpu.make_async_copy(src, dst.at[core], dp_local.at[n])
        here.start()
        copies.append((there, here))

    def in_wait(n):
        dst = moved[n][1]
        for side in range(2):
            ref = dst.at[pl.ds(side * HALF, HALF)]

            @pl.when(owners[side] != me)
            def _():
                arrived(ref, in_send.at[n, 0], in_recv.at[n, side], {"ctx": owners[side]})

            @pl.when(owners[side] == me)
            def _():
                pltpu.make_async_copy(ref, ref, in_local.at[n]).wait()

    def dp_wait(n):
        copies[n][1].wait()
        arrived(weights[n][1].at[1 - core], dp_send.at[n], dp_recv.at[n], other)

    in_wait(0)
    in_wait(1)
    dp_wait(0)
    gain1 = jnp.concatenate([gains[0, 0:1, 0:288], gains[1, 0:1, 0:288]], axis=1)
    gain2 = jnp.concatenate([gains[0, 1:2, 0:288], gains[1, 1:2, 0:288]], axis=1)
    x = xz[...].astype(F32)
    h1f, _ = rms_forward(x, gain1)
    h1 = h1f.astype(BF16)
    h1_kept[...] = h1
    for n in (1, 2):
        dp_wait(n)

    def whole(ref):
        return ref[...].reshape(D, ref.shape[-1])

    cosines, sines = trig[:, 0:HEAD], trig[:, HEAD : 2 * HEAD]
    k_lin = nn(h1, whole(wk))
    v_lin = nn(h1, whole(wv))
    for h in every:
        cols = slice(h * HEAD, (h + 1) * HEAD)
        key = k_lin[:, cols]
        key = key * cosines + swap_halves(key) * sines
        kv[h, place.at[2], place.at[1], place.at[0]] = jnp.concatenate([key, v_lin[:, cols]], axis=1).astype(BF16)
    keys_gather = gather_task(place, kv, 0, ROWS, as_, ar)
    next(keys_gather)
    dp_wait(3)
    q_lin = nn(h1, whole(wq))
    for h in range(HEADS):
        query = q_lin[:, h * HEAD : (h + 1) * HEAD]
        query = (query * cosines + swap_halves(query) * sines).astype(BF16)
        query = (query.astype(F32) * HEAD**-0.5).astype(BF16)
        query = jnp.concatenate([query, jnp.zeros((ROWS, HEAD), BF16)], axis=1)
        group = (h % GROUPS) * HALF
        qpad[h // GROUPS, group : group + HALF] = query[:HALF]
        qpad[h // GROUPS, 192 + group : 192 + group + HALF] = query[HALF:]
    for _ in range(4):
        next(keys_gather)

    slab = place.at[2]
    inner = lax.rem(me, 16)
    late_rows = slice(192, 384)

    def spot(h, p, z, piece, side):
        rows = slice(side * HALF, (side + 1) * HALF)
        if h == 0:
            return (0, z, pl.ds(2 * piece, 2), slice(None), rows)
        if h == 1:
            return (1, z, slice(None), place.coord(0, p), rows)
        return (2, z, place.coord(1, p), slice(None), rows)

    def keys_at(h, p, z, piece, side):
        block = kv[spot(h, p, z, piece, side)]
        return block.reshape(-1, 128)

    def masks(h, p, piece):
        count = 512 if h == 0 else 256
        row = lax.broadcasted_iota(jnp.int32, (count, 384), 0)
        lane = lax.broadcasted_iota(jnp.int32, (count, 384), 1)
        block = row // HALF
        if h == 0:
            block = block + 8 * piece
        elif h == 1:
            block = 4 * block + place.coord(0, p)
        else:
            block = block + 4 * place.coord(1, p)
        token, query = lax.rem(row, HALF), lax.rem(lane, HALF)
        low = token + HALF * block <= jnp.where(lane < 192, HALF * inner + query, HALF * 64)
        high = token - HALF * block <= query - HALF * inner
        return low, high[:, :192]

    def by_plane(p, heads_of):
        def slabs(z, units):
            for kind, when in ((0, z < slab), (1, z == slab), (2, z > slab)):

                @pl.when(when)
                def _():
                    heads_of(units, z, kind)

        def one(z, _):
            slabs(z, ((1, 0), (2, 0)))
            return 0

        if p == 0:
            for piece in range(2):
                heads_of(((0, piece),), slab, 1)
        else:
            z = place.coord(2, p)
            for kind, when in ((0, z < slab), (2, z > slab)):

                @pl.when(when)
                def _():
                    heads_of(((0, 0), (0, 1)), z, kind)

        lax.fori_loop(0, 4, one, 0)

    def forward_step(block, queries, mask, state):
        top, accum = state
        scores = nt(block, queries)
        if mask is not None:
            scores = jnp.where(mask, scores, MASKED)
        new_top = jnp.maximum(top, jnp.max(scores, axis=0, keepdims=True))
        weights = jnp.exp(scores - new_top).astype(BF16)
        ones_lane = lax.broadcasted_iota(jnp.int32, block.shape, 1) < HEAD
        values = jnp.where(ones_lane, jnp.ones_like(block), block)
        return new_top, accum * jnp.exp(top - new_top) + tn(values, weights)

    def forward_plane(p):
        def heads_of(units, z, kind):
            for h, piece in units:
                low, high = masks(h, p, piece) if kind == 1 else (None, None)
                if kind < 2:
                    state = (top_ab[h], acc_ab[h])
                    top_ab[h], acc_ab[h] = forward_step(keys_at(h, p, z, piece, 0), qpad[h], low, state)
                if kind > 0:
                    block = keys_at(h, p, z, piece, 1)
                    if kind == 2:
                        block = jnp.concatenate([keys_at(h, p, z, piece, 0), block], axis=0)
                    state = (top_b[h], acc_b[h])
                    top_b[h], acc_b[h] = forward_step(block, qpad[h, late_rows], high, state)

        by_plane(p, heads_of)

    top_ab[...] = jnp.full_like(top_ab, MASKED)
    top_b[...] = jnp.full_like(top_b, MASKED)
    acc_ab[...] = jnp.zeros_like(acc_ab)
    acc_b[...] = jnp.zeros_like(acc_b)
    forward_plane(0)
    next(keys_gather)
    next(keys_gather)
    forward_plane(1)
    forward_plane(3)
    next(keys_gather)
    forward_plane(2)
    in_wait(2)
    for n in (4, 5, 6, 7):
        dp_wait(n)
    for h in every:
        top = jnp.maximum(top_ab[h][:, 192:], top_b[h])
        accum = acc_ab[h][:, 192:] * jnp.exp(top_ab[h][:, 192:] - top) + acc_b[h] * jnp.exp(top_b[h] - top)
        top = jnp.concatenate([top_ab[h][:, :192], top], axis=1)
        accum = jnp.concatenate([acc_ab[h][:, :192], accum], axis=1)
        total = accum[0:1, :]
        outs = accum / total
        outs_t[h] = outs
        lse[h] = top + jnp.log(total)
        attn[h] = outs.T.astype(BF16)

    def by_token(ref, lanes):
        pieces = []
        for h in range(HEADS):
            group = (h % GROUPS) * HALF
            here = ref[h // GROUPS]
            pieces.append(jnp.concatenate([here[group : group + HALF, lanes], here[192 + group : 192 + group + HALF, lanes]], axis=0))
        return jnp.concatenate(pieces, axis=1)

    attn_low = by_token(attn, slice(64, 128))

    def put(buf, rows, base, length, value, half):
        for tile in range(value.shape[1] // 128):
            at, done = base + tile * length, 0
            while done < value.shape[0]:
                chunk, row = (at + done) // rows, (at + done) % rows
                size = min(rows - row, value.shape[0] - done)
                spot = (chunk // 4 % 4, chunk % 4, slice(row, row + size))
                if len(buf.shape) == 7:
                    spot = (chunk // 64, chunk // 16 % 4, *spot)
                buf[(half, *spot)] = value[done : done + size, tile * 128 : (tile + 1) * 128].astype(BF16)
                done += size

    def gain_line(grad, half):
        line = jnp.concatenate([grad[:, 288 * half : 288 * (half + 1)], jnp.zeros((1, 96), F32)], axis=1)
        return jnp.concatenate([line[:, 128 * k : 128 * (k + 1)] for k in range(3)] + [jnp.zeros((13, 128), F32)], axis=0)

    x2 = x + nn(attn_low, whole(wo))
    h2f, inverse2 = rms_forward(x2, gain2)
    h2 = h2f.astype(BF16)
    pad = jnp.zeros((ROWS, 64), BF16)
    dy_low = cotz[...]
    total = x2
    grad_h2 = jnp.zeros((ROWS, D), F32)
    for t in range(2):
        cols = slice(768 * t, 768 * (t + 1))
        wg_t, wu_t = wg[:, :, cols].reshape(D, 768), wu[:, :, cols].reshape(D, 768)
        gate = nn(h2, wg_t)
        up = nn(h2, wu_t)
        sigma = jax.nn.sigmoid(gate)
        active = gate * sigma
        hidden = (active * up).astype(BF16)
        total = total + nt(hidden, wd[t])
        grad_hidden = nn(dy_low, wd[t])
        grad_gate = (grad_hidden * up * (sigma + active * (1.0 - sigma))).astype(BF16)
        grad_up = (grad_hidden * active).astype(BF16)
        grad_h2 = grad_h2 + nt(grad_gate, wg_t) + nt(grad_up, wu_t)
        for base, value in ((E_GATE, tn(h2, grad_gate)), (E_UP, tn(h2, grad_up))):
            for half in range(2):
                put(e_all, 64, base + 6 * t * 288, 288, value[288 * half : 288 * (half + 1)], half)
        put(e_all, 64, E_DOWN, 576, tn(dy_low, hidden), t)
    for part in range(2):
        send(e_all.at[1 - core, part], e_peer.at[part], dps.at[part], dpr.at[part], other)
    result[...] = total.astype(BF16)
    grad_norm2, grad_gain2 = rms_backward(x2, inverse2, gain2, grad_h2)
    grad_x2 = dy_low.astype(F32) + grad_norm2
    grad_x2_kept[...] = grad_x2
    grad_attn = grad_x2.astype(BF16)
    grad_out = tn(attn_low, jnp.concatenate([grad_attn, pad], axis=1))
    for half in range(2):
        put(e_all, 64, E_OUT, 288, grad_out[288 * half : 288 * (half + 1)], half)
        put(e_all, 64, E_GAIN, 16, gain_line(grad_gain2, half), half)
        put(e_all, 64, E_GAIN + 16, 0, jnp.zeros((E_ROWS - E_GAIN - 16, 128), F32), half)
    send(e_all.at[1 - core, 2], e_peer.at[2], dps.at[2], dpr.at[2], other)

    def out_copy(n, side, here=False):
        src, dst = ((result, out_result), (grad_z, out_grad))[n]
        k = lax.rem((me, 127 - me)[side], 2)
        a = src.at[pl.ds(side * HALF, HALF)]
        b = dst.at[pl.ds(pl.multiple_of(k * HALF, HALF), HALF)]
        if here:
            return pltpu.make_async_copy(a, b, zl.at[n])
        return remote(a, b, zs.at[n, side], zr.at[n, k], {"ctx": owners[side]})

    def out_send(n):
        for side in range(2):

            @pl.when(owners[side] != me)
            def _():
                out_copy(n, side).start()

            @pl.when(owners[side] == me)
            def _():
                out_copy(n, side, here=True).start()

    def out_wait(n):
        dst = (out_result, out_grad)[n]
        for k in range(2):
            ref = dst.at[pl.ds(k * HALF, HALF)]

            @pl.when(targets[k] != me)
            def _():
                arrived(ref, zs.at[n, 0], zr.at[n, k], {"ctx": targets[k]})

            @pl.when(targets[k] == me)
            def _():
                pltpu.make_async_copy(ref, ref, zl.at[n]).wait()

        for side in range(2):

            @pl.when(owners[side] != me)
            def _():
                out_copy(n, side).wait_send()

    out_send(0)
    e_work = e_all.at[core]

    def early():
        for part in range(3):
            remote(e_all.at[1 - core, part], e_peer.at[part], dps.at[part], dpr.at[part], other).wait()
            for z in range(4):
                index = (core, part, z)
                e_all[index] = (e_all[index].astype(F32) + e_peer[part, z].astype(F32)).astype(BF16)

        def e_keep(part, index, total):
            e_sum[index] = total.astype(BF16)

        yield from scatter_task(place, e_work, (eh0, eh1, eh2), (ew0, ew1, ew2), 64, es, er, e_keep)
        yield from gather_task(place, e_sum, 0, 64, gs, gr)

    early_task = early()

    grad_o = nt(grad_attn, whole(wo)).astype(BF16)
    for h in range(HEADS):
        piece = grad_o[:, h * HEAD : (h + 1) * HEAD]
        piece = jnp.concatenate([jnp.zeros((ROWS, HEAD), BF16), piece], axis=1)
        group = (h % GROUPS) * HALF
        dopad[h // GROUPS, group : group + HALF] = piece[:HALF]
        dopad[h // GROUPS, 192 + group : 192 + group + HALF] = piece[HALF:]

    deltas = [jnp.sum(dopad[h].astype(F32).T * outs_t[h], axis=0, keepdims=True) for h in every]
    logs = [lse[h] for h in every]

    def backward_step(block, queries, grads, log_total, delta, mask, grad_q):
        scores = nt(block, queries)
        if mask is not None:
            scores = jnp.where(mask, scores, MASKED)
        probs = jnp.exp(scores - log_total)
        grad_scores = (probs * (nt(block, grads) - delta)).astype(BF16)
        part = nn(grad_scores, queries) + nn(probs.astype(BF16), grads)
        return grad_q + tn(block, grad_scores), part.astype(BF16)

    dq_early[...] = jnp.zeros_like(dq_early)
    dq_late[...] = jnp.zeros_like(dq_late)

    def backward_plane(p):
        def heads_of(units, z, kind):
            for h, piece in units:
                low, high = masks(h, p, piece) if kind == 1 else (None, None)
                early_spot, late_spot = (spot(h, p, z, piece, side) for side in range(2))

                def save(at, part):
                    dkv[at] = part.reshape(-1, 4, HALF, 128) if h == 0 else part.reshape(4, HALF, 128)

                if kind < 2:
                    block = keys_at(h, p, z, piece, 0)
                    dq_early[h], part = backward_step(block, qpad[h], dopad[h], logs[h], deltas[h], low, dq_early[h])
                    save(early_spot, part)
                if kind == 0:
                    save(late_spot, jnp.zeros_like(part))
                else:
                    block = keys_at(h, p, z, piece, 1)
                    size = block.shape[0]
                    if kind == 2:
                        block = jnp.concatenate([keys_at(h, p, z, piece, 0), block], axis=0)
                    dq_late[h], part = backward_step(
                        block, qpad[h, late_rows], dopad[h, late_rows], logs[h][:, 192:], deltas[h][:, 192:],
                        high, dq_late[h],
                    )
                    if kind == 2:
                        save(early_spot, part[:size])
                        part = part[size:]
                    save(late_spot, part)

        by_plane(p, heads_of)

    def keep(part, index, total):
        own[part] = total

    keys_task = scatter_task(place, dkv, (kh0, kh1, kh2), (kw0, kw1, kw2), ROWS, ks, kr, keep, stepwise=True)
    backward_plane(2)
    next(keys_task)
    next(early_task)
    backward_plane(1)
    next(early_task)
    backward_plane(3)
    next(keys_task)
    next(early_task)
    next(keys_task)
    backward_plane(0)
    next(early_task)
    for h in every:
        dq_rows[h] = jnp.concatenate([dq_early[h][:, :192], dq_early[h][:, 192:] + dq_late[h]], axis=1).T
    grad_q = by_token(dq_rows, slice(0, 64)) * HEAD**-0.5
    pieces = []
    for h in range(HEADS):
        piece = grad_q[:, h * HEAD : (h + 1) * HEAD]
        pieces.append(piece * cosines - swap_halves(piece) * sines)
    dq_low = jnp.concatenate(pieces, axis=1).astype(BF16)
    grad_query = tn(h1_kept[...], jnp.concatenate([dq_low, pad], axis=1))
    for half in range(2):
        put(m_full, 96, 0, 288, grad_query[288 * half : 288 * (half + 1)], half)
        put(m_full, 96, 1440, 0, jnp.zeros((96, 128), F32), half)
    m_copy = send(m_full.at[1 - core], m_peer, dps.at[3], dpr.at[3], other)
    grad_h1_q = nt(dq_low, whole(wq))

    def middle_part():
        yield
        arrived(m_peer, dps.at[3], dpr.at[3], other)
        m_work[...] = (m_full[core].astype(F32) + m_peer[...].astype(F32)).astype(BF16)
        yield from plane_sum_task(place, m_work, m_slots, m_layers, m_sum, (m0, m1, m2, m3, m4, m5))
        m_copy.wait_send()

    def late_part():
        yield from keys_task
        keys, values = [], []
        for h in every:
            piece = own[h]
            grad_k = piece[:, :HEAD]
            keys.append(grad_k * cosines - swap_halves(grad_k) * sines)
            values.append(piece[:, HEAD:])
        dk_low = jnp.concatenate(keys, axis=1).astype(BF16)
        dv_low = jnp.concatenate(values, axis=1).astype(BF16)
        weight_grads = tn(h1_kept[...], jnp.concatenate([dk_low, dv_low], axis=1))
        grad_h1 = grad_h1_q + nt(dk_low, whole(wk)) + nt(dv_low, whole(wv))
        x = xz[...].astype(F32)
        inverse1 = lax.rsqrt(jnp.mean(x * x, axis=-1, keepdims=True) + EPS)
        grad_norm1, grad_gain1 = rms_backward(x, inverse1, gain1, grad_h1)
        for half in range(2):
            put(l_full, 64, 0, 288, weight_grads[288 * half : 288 * (half + 1)], half)
            put(l_full, 64, 864, 16, gain_line(grad_gain1, half), half)
            put(l_full, 64, 880, 0, jnp.zeros((144, 128), F32), half)
        l_copy = send(l_full.at[1 - core], l_peer, dps.at[4], dpr.at[4], other)
        grad_z[...] = (grad_x2_kept[...] + grad_norm1).astype(BF16)
        out_send(1)
        yield
        arrived(l_peer, dps.at[4], dpr.at[4], other)
        l_work[...] = (l_full[core].astype(F32) + l_peer[...].astype(F32)).astype(BF16)
        yield from plane_sum_task(place, l_work, l_slots, l_layers, l_sum, (l0, l1, l2, l3, l4, l5))
        l_copy.wait_send()

    run_together(late_part(), early_task, middle_part(), keys_gather)
    out_wait(0)
    out_wait(1)
    for there, _ in copies:
        there.wait_send()
    for n in range(3):
        for k in range(2):

            @pl.when(targets[k] != me)
            def _():
                in_copy(n, k).wait_send()


def layer_call(x, trig, cot, gain1, gain2, weights):
    def buffers(rows):
        dims = ((4, 4), (4,), ())
        halves = [pltpu.VMEM((3, 2, *d, rows // 2, 128), BF16) for d in dims]
        wholes = [pltpu.VMEM((3, 2, *d, rows, 128), BF16) for d in dims]
        return halves + wholes

    def summed(rows):
        dims = ((2, 4, 4), (4, 4), (4, 4), (15,), (4,))
        return [pltpu.VMEM((*d, rows, 128), BF16) for d in dims]

    sem = pltpu.SemaphoreType.DMA
    v = pltpu.VMEM
    return pl.pallas_call(
        layer_kernel,
        out_shape=(
            shape((3, 4, 4, 4, 64, 128), BF16), shape((4, 4, 96, 128), BF16), shape((4, 4, 64, 128), BF16),
            shape((ROWS, D), BF16), shape((ROWS, D), BF16),
        ),
        in_specs=(*vmem(5), *anywhere(7)),
        out_specs=tuple(vmem(5)),
        scratch_shapes=[
            v((ROWS, D), BF16), v((ROWS, D), BF16), v((8, 384), F32),
            v((ROWS, D), BF16), v((ROWS, 128), F32), v((ROWS, D), BF16), v((2, 8, 384), F32),
            *[v((2, *w.shape), BF16) for w in weights],
            v((ROWS, D), BF16), v((KV_HEADS, 384, 128), BF16), v((KV_HEADS, 4, 4, 4, ROWS, 128), BF16),
            v((KV_HEADS, 1, 384), F32), v((KV_HEADS, 128, 384), F32), v((KV_HEADS, 1, 192), F32), v((KV_HEADS, 128, 192), F32),
            v((KV_HEADS, 128, 384), F32), v((KV_HEADS, 1, 384), F32), v((KV_HEADS, 384, 128), BF16),
            v((KV_HEADS, 384, 128), BF16), v((KV_HEADS, 128, 384), F32), v((KV_HEADS, 128, 192), F32),
            v((KV_HEADS, 384, 128), F32), v((ROWS, D), BF16), v((ROWS, D), F32),
            v((3, 4, 4, 4, ROWS, 128), BF16), v((2, 3, 4, 4, 4, 64, 128), BF16), v((3, 4, 4, 4, 64, 128), BF16),
            *summed(96), *summed(64),
            v((3, ROWS, 128), F32), v((ROWS, D), BF16),
            *buffers(ROWS), *buffers(64),
            sem((3, 2)), sem((3, 2)), sem((3,)), sem((8,)), sem((8,)), sem((8,)), sem((3, 3, 6)), sem((3, 3, 6)),
            sem((3, 3, 6)), sem((3, 3, 6)), sem((3, 3, 6)), sem((3, 3, 6)), sem((3, 3, 6)), sem((3, 3, 6)),
            *[sem((n,)) for n in (15, 15, 3, 3, 15, 15) * 2],
            sem((5,)), sem((5,)), sem((2, 2)), sem((2, 2)), sem((2,)),
        ],
        compiler_params=pltpu.CompilerParams(collective_id=0, has_side_effects=True, vmem_limit_bytes=VMEM_LIMIT),
        name="decoder_layer",
    )(x, trig, cot, gain1, gain2, *weights)


def unpack_kernel(e, m, l, result, grad, result_t, grad_t, gain1, gq, gk, gv, go, gain2, gg, gu, gd):
    def take(ref, base, length, out):
        columns = out.shape[1]
        for tile in range(-(-columns // 128)):
            wide = min(128, columns - 128 * tile)
            at = base + tile * length
            out[:, 128 * tile : 128 * tile + wide] = ref[at : at + length, :wide].astype(F32)

    take(e, E_GATE, 288, gg)
    take(e, E_UP, 288, gu)
    take(e, E_DOWN, 576, gd)
    result_t[...] = result[...].T
    grad_t[...] = grad[...].T
    take(e, E_OUT, 288, go)
    take(m, 0, 288, gq)
    whole = jnp.concatenate([l[tile * 288 : (tile + 1) * 288, :] for tile in range(3)], axis=1).astype(F32)
    gk[...] = whole[:, 0:192]
    gv[...] = whole[:, 192:384]
    for ref, at, gain in ((e, E_GAIN, gain2), (l, 864, gain1)):
        lines = ref[at : at + 16, :].astype(F32)
        gain[...] = jnp.concatenate([lines[k : k + 1, :] for k in range(3)], axis=1)[:, :288].reshape(288)


def unpack_call(e, m, l, result, grad):
    return pl.pallas_call(
        unpack_kernel,
        out_shape=(
            shape((D, ROWS), BF16), shape((D, ROWS), BF16),
            shape((288,), F32), shape((288, D), F32), shape((288, 192), F32), shape((288, 192), F32),
            shape((288, D), F32), shape((288,), F32), shape((288, FF), F32), shape((288, FF), F32), shape((D, 768), F32),
        ),
        in_specs=vmem(5),
        out_specs=tuple(vmem(11)),
        compiler_params=pltpu.CompilerParams(vmem_limit_bytes=VMEM_LIMIT),
        name="unpack_gradients",
    )(e, m, l, result, grad)


def body(
    layer_in, positions, norm_gain1, w_query, w_key, w_value, w_out, norm_gain2, w_gate, w_up, w_down, cotangent
):
    inv_freq = np.tile(10000.0 ** (-np.arange(HEAD // 2) / (HEAD // 2)), 4).astype(np.float32)
    angles = positions[0].astype(F32)[:, None] * inv_freq[None, :]
    lane = lax.broadcasted_iota(jnp.int32, (ROWS, 128), 1)
    sines = jnp.sin(angles)
    trig = jnp.where(lane < 64, jnp.cos(angles), jnp.where(lane < 96, -sines, sines))
    e_sum, m_sum, l_sum, result, grad = layer_call(
        layer_in[0].T, trig, cotangent[0].T, norm_gain1, norm_gain2,
        (w_query, w_key, w_value, w_out, w_gate, w_up, w_down.T),
    )
    result, grad, gain1, gq, gk, gv, go, gain2, gg, gu, gd = unpack_call(
        e_sum.reshape(-1, 128), m_sum.reshape(-1, 128), l_sum.reshape(-1, 128), result, grad
    )
    return (result.T[None], grad.T[None], gain1, gq, gk, gv, go, gain2, gg, gu, gd.T)


def solution(mesh):
    weight = P("dp", None)
    tokens = P("dp", "ctx", None)
    return jax.shard_map(
        body,
        mesh=mesh,
        in_specs=(tokens, P("dp", "ctx"), P("dp"), weight, weight, weight, weight, P("dp"), weight, weight, weight, tokens),
        out_specs=(tokens, tokens, P("dp"), weight, weight, weight, weight, P("dp"), weight, weight, weight),
        check_vma=False,
    )
```

```python
import jax
import jax.numpy as jnp
import numpy as np
from jax import lax
from jax.experimental import pallas as pl
from jax.experimental.pallas import tpu as pltpu
from jax.sharding import PartitionSpec as P

HEADS = 9
KV_HEADS = 3
GROUPS = HEADS // KV_HEADS
HEAD = 64
D = 576
FF = 1536
EPS = 1e-05
MASKED = -1e30
HALF = 64
ROWS = 2 * HALF
MESH = pl.DeviceIdType.MESH
F32 = jnp.float32
BF16 = jnp.bfloat16
VMEM_LIMIT = 60 * 1024 * 1024

E_GATE = 0
E_UP = 12 * 288
E_DOWN = 24 * 288
E_OUT = E_DOWN + 6 * 576
E_GAIN = E_OUT + 5 * 288
E_ROWS = 3 * 64 * 64


def vmem(n):
    return [pl.BlockSpec(memory_space=pltpu.VMEM)] * n


def anywhere(n):
    return [pl.BlockSpec(memory_space=pl.ANY)] * n


def shape(dims, dtype):
    return jax.ShapeDtypeStruct(dims, dtype)


def nn(a, b):
    return jnp.dot(a, b, preferred_element_type=F32)


def nt(a, b):
    return lax.dot_general(a, b, (((1,), (1,)), ((), ())), preferred_element_type=F32)


def tn(a, b):
    return lax.dot_general(a, b, (((0,), (0,)), ((), ())), preferred_element_type=F32)


def run_together(*tasks):
    tasks = list(tasks)
    while tasks:
        for task in list(tasks):
            try:
                next(task)
            except StopIteration:
                tasks.remove(task)


class Place:
    def __init__(self):
        self.core = lax.axis_index("dp")
        self.me = lax.axis_index("ctx")
        self.at = [lax.rem(self.me // 4**a, 4) for a in range(3)]
        self.coords = [[lax.rem(self.at[a] + step, 4) for step in range(4)] for a in range(3)]
        self.plane = [(dy, dx) for dy in range(4) for dx in range(4) if dy or dx]
        self.devices = [[self.me + (self.coords[a][step] - self.at[a]) * 4**a for step in range(4)] for a in range(3)]

    def toward(self, axis, step):
        return self.devices[axis][step]

    def in_plane(self, dy, dx):
        return self.devices[1][dy] + self.devices[0][dx] - self.me

    def coord(self, axis, step):
        return self.coords[axis][step]

    def region(self, part, phase, coord):
        index = [None, None, None]
        for k in range(3):
            axis = (part + k) % 3
            index[2 - axis] = pl.ds(0, 4) if k < phase else coord if k == phase else self.at[axis]
        return tuple(index)


def remote(src, dst, send_sem, recv_sem, device):
    return pltpu.make_async_remote_copy(
        src_ref=src, dst_ref=dst, send_sem=send_sem, recv_sem=recv_sem, device_id=device, device_id_type=MESH
    )


def send(src, dst, send_sem, recv_sem, device):
    copy = remote(src, dst, send_sem, recv_sem, device)
    copy.start()
    return copy


class Sends:
    def __init__(self):
        self.made = []

    def start(self, src, src_at, dst, dst_at, send_sem, recv_sem, at, device):
        def make():
            return remote(src.at[src_at], dst.at[dst_at], send_sem.at[at], recv_sem.at[at], device)

        make().start()
        self.made.append(make)

    def wait(self):
        for make in self.made:
            make().wait_send()


def arrived(dst, send_sem, recv_sem, device):
    pltpu.make_async_remote_copy(
        src_ref=dst, dst_ref=dst, send_sem=send_sem, recv_sem=recv_sem, device_id=device, device_id_type=MESH
    ).wait_recv()


def gather_task(place, buf, row, rows, ssem, rsem):
    first, second = pl.ds(row, rows // 2), pl.ds(row + rows // 2, rows // 2)
    sent = Sends()
    for phase in range(3):
        for part in range(3):
            axis = (part + phase) % 3
            plus, minus = {"ctx": place.toward(axis, 1)}, {"ctx": place.toward(axis, 3)}
            own = place.region(part, phase, place.at[axis])
            for k, (half, to) in enumerate(((first, plus), (second, minus), (second, plus), (first, minus))):
                index = (part, *own, half)
                sent.start(buf, index, buf, index, ssem, rsem, (part, phase, k), to)
        yield
        for part in range(3):
            axis = (part + phase) % 3
            plus, minus = {"ctx": place.toward(axis, 1)}, {"ctx": place.toward(axis, 3)}
            for k, (half, step, to) in enumerate(((first, 3, plus), (second, 1, minus))):
                index = (part, *place.region(part, phase, place.coord(axis, step)), half)
                arrived(buf.at[index], ssem.at[part, phase, k], rsem.at[part, phase, k], to)
                sent.start(buf, index, buf, index, ssem, rsem, (part, phase, 4 + k), to)
        yield
        for part in range(3):
            axis = (part + phase) % 3
            plus = {"ctx": place.toward(axis, 1)}
            for k, half, step in ((2, second, 3), (3, first, 1)):
                ref = buf.at[(part, *place.region(part, phase, place.coord(axis, step)), half)]
                arrived(ref, ssem.at[part, phase, k], rsem.at[part, phase, k], plus)
        if phase == 2:
            yield
        for part in range(3):
            axis = (part + phase) % 3
            plus = {"ctx": place.toward(axis, 1)}
            for k, half, step in ((4, first, 2), (5, second, 2)):
                ref = buf.at[(part, *place.region(part, phase, place.coord(axis, step)), half)]
                arrived(ref, ssem.at[part, phase, k], rsem.at[part, phase, k], plus)
    yield
    sent.wait()


def add_into(buf, index, other):
    buf[index] = (buf[index].astype(F32) + other.astype(F32)).astype(BF16)


def scatter_task(place, buf, halves, wholes, rows, ssem, rsem, finish, stepwise=False):
    first, second = pl.ds(0, rows // 2), pl.ds(rows // 2, rows // 2)
    sent = Sends()
    for turn in range(3):
        phase = 2 - turn
        half_buf, whole_buf = halves[turn], wholes[turn]
        for near in range(2):
            for part in range(3):
                axis = (part + phase) % 3
                plus, minus = {"ctx": place.toward(axis, 1)}, {"ctx": place.toward(axis, 3)}
                far = place.region(part, phase, place.coord(axis, 2))
                right = place.region(part, phase, place.coord(axis, 1))
                left = place.region(part, phase, place.coord(axis, 3))
                lead = (slice(None),) * phase
                for k, src, dst, to in (
                    (0, (*far, first), (half_buf, (part, 0)), plus),
                    (1, (*far, second), (half_buf, (part, 1)), minus),
                    (2, (*right, second), (whole_buf, (part, 0, *lead, second)), plus),
                    (3, (*left, first), (whole_buf, (part, 1, *lead, first)), minus),
                )[2 * near : 2 * near + 2]:
                    sent.start(buf, (part, *src), *dst, ssem, rsem, (part, turn, k), to)
            if stepwise and turn == 0 and near == 0:
                yield
        yield
        for part in range(3):
            axis = (part + phase) % 3
            plus, minus = {"ctx": place.toward(axis, 1)}, {"ctx": place.toward(axis, 3)}
            lead = (slice(None),) * phase
            for k, half, step, to in ((0, first, 1, plus), (1, second, 3, minus)):
                arrived(half_buf.at[part, k], ssem.at[part, turn, k], rsem.at[part, turn, k], to)
                index = (part, *place.region(part, phase, place.coord(axis, step)), half)
                add_into(buf, index, half_buf[part, k])
                sent.start(buf, index, whole_buf, (part, k, *lead, half), ssem, rsem, (part, turn, 4 + k), to)
        yield
        for part in range(3):
            axis = (part + phase) % 3
            plus = {"ctx": place.toward(axis, 1)}
            lead = (slice(None),) * phase
            for k, side, half in ((2, 0, second), (3, 1, first), (4, 0, first), (5, 1, second)):
                dst = whole_buf.at[(part, side, *lead, half)]
                arrived(dst, ssem.at[part, turn, k], rsem.at[part, turn, k], plus)
            index = (part, *place.region(part, phase, place.at[axis]))
            total = buf[index].astype(F32) + whole_buf[part, 0].astype(F32) + whole_buf[part, 1].astype(F32)
            if turn < 2:
                buf[index] = total.astype(BF16)
            else:
                finish(part, index, total)
    yield
    sent.wait()


def plane_sum_task(place, buf, slots, layers, out, sems):
    sent = Sends()
    here = (place.at[1], place.at[0])
    there, back, peers = [], [], []
    for dy, dx in place.plane:
        there.append((place.coord(1, dy), place.coord(0, dx)))
        back.append((place.coord(1, (4 - dy) % 4), place.coord(0, (4 - dx) % 4)))
        peers.append({"ctx": place.in_plane(dy, dx)})
    for k, to in enumerate(peers):
        sent.start(buf, there[k], slots, k, sems[0], sems[1], k, to)
    yield
    total = buf[here].astype(F32)
    for k, to in enumerate(peers):
        arrived(slots.at[k], sems[0].at[k], sems[1].at[k], to)
        total = total + slots[k].astype(F32)
    layers[place.at[2]] = total.astype(BF16)
    for k in range(3):
        to = {"ctx": place.toward(2, k + 1)}
        sent.start(layers, place.at[2], layers, place.at[2], sems[2], sems[3], k, to)
    yield
    for k in range(3):
        to = {"ctx": place.toward(2, k + 1)}
        arrived(layers.at[place.coord(2, 3 - k)], sems[2].at[k], sems[3].at[k], to)
    total = layers[0].astype(F32)
    for z in range(1, 4):
        total = total + layers[z].astype(F32)
    out[here] = total.astype(BF16)
    for k, to in enumerate(peers):
        sent.start(out, here, out, here, sems[4], sems[5], k, to)
    yield
    for k, to in enumerate(peers):
        arrived(out.at[back[k]], sems[4].at[k], sems[5].at[k], to)
    yield
    sent.wait()


def greet(place, partners):
    barrier = pltpu.get_barrier_semaphore()
    for step in (1, 2, 3):
        pl.semaphore_signal(barrier, inc=1, device_id={"ctx": place.toward(2, step)}, device_id_type=MESH)
    for dy, dx in place.plane:
        pl.semaphore_signal(barrier, inc=1, device_id={"ctx": place.in_plane(dy, dx)}, device_id_type=MESH)
    pl.semaphore_signal(barrier, inc=1, device_id={"dp": 1 - place.core}, device_id_type=MESH)
    count = 19
    for partner in partners:

        @pl.when(partner != place.me)
        def _():
            pl.semaphore_signal(barrier, inc=1, device_id={"ctx": partner}, device_id_type=MESH)

        count = count + jnp.where(partner != place.me, 1, 0)
    pl.semaphore_wait(barrier, count)


def folded(half_block):
    return jnp.where(half_block < 64, half_block, 127 - half_block)


def swap_halves(v):
    return jnp.concatenate([v[:, HEAD // 2 :], v[:, : HEAD // 2]], axis=1)


def rms_forward(values, gain):
    inverse = lax.rsqrt(jnp.mean(values * values, axis=-1, keepdims=True) + EPS)
    return values * inverse * gain, inverse


def rms_backward(values, inverse, gain, grad):
    normal = values * inverse
    grad_gain = jnp.sum(grad * normal, axis=0, keepdims=True)
    scaled = grad * gain
    grad_in = inverse * (scaled - normal * jnp.mean(scaled * normal, axis=-1, keepdims=True))
    return grad_in, grad_gain


def layer_kernel(
    x_in, trig_in, cot_in, gain1_in, gain2_in, wq_in, wk_in, wv_in, wo_in, wg_in, wu_in, wd_in,
    e_sum, m_sum, l_sum, out_result, out_grad,
    x_rows, cot_rows, g_rows, xz, trig, cotz, gains, wq, wk, wv, wo, wg, wu, wd, h1_kept, qpad, kv,
    top_ab, acc_ab, top_b, acc_b, outs_t, lse, dopad, attn, dq_early, dq_late, dq_rows, result, grad_x2_kept,
    dkv, e_all, e_peer, m_full, m_peer, m_work, m_slots, m_layers, l_full, l_peer, l_work, l_slots, l_layers, own, grad_z,
    kh0, kh1, kh2, kw0, kw1, kw2, eh0, eh1, eh2, ew0, ew1, ew2,
    in_send, in_recv, in_local, dp_send, dp_recv, dp_local, as_, ar,
    ks, kr, es, er, gs, gr, m0, m1, m2, m3, m4, m5, l0, l1, l2, l3, l4, l5, dps, dpr, zs, zr, zl,
):
    place = Place()
    me, core = place.me, place.core
    every = range(KV_HEADS)

    x_rows[...] = x_in[...].T
    g_rows[...] = jnp.zeros((8, 384), F32)
    g_rows[0:1, 0:288] = gain1_in[...].astype(F32).reshape(1, 288)
    g_rows[1:2, 0:288] = gain2_in[...].astype(F32).reshape(1, 288)
    cot_rows[...] = cot_in[...].T
    targets = [folded(2 * me + k) for k in range(2)]
    owners = [me // 2, (127 - me) // 2]
    greet(place, owners + targets)
    slot = me // 32
    moved = ((x_rows, xz), (trig_in, trig), (cot_rows, cotz))

    def in_copy(n, k, here=False):
        src, dst = moved[n]
        a, b = src.at[pl.ds(HALF * k, HALF)], dst.at[pl.ds(pl.multiple_of(slot * HALF, HALF), HALF)]
        if here:
            return pltpu.make_async_copy(a, b, in_local.at[n])
        return remote(a, b, in_send.at[n, k], in_recv.at[n, slot], {"ctx": targets[k]})

    for n in range(3):
        for k in range(2):

            @pl.when(targets[k] != me)
            def _():
                in_copy(n, k).start()

            @pl.when(targets[k] == me)
            def _():
                in_copy(n, k, here=True).start()

    other = {"dp": 1 - core}
    weights = ((g_rows, gains), (wk_in, wk), (wv_in, wv), (wq_in, wq), (wo_in, wo), (wg_in, wg), (wu_in, wu), (wd_in, wd))
    copies = []
    for n, (src, dst) in enumerate(weights):
        there = send(src, dst.at[core], dp_send.at[n], dp_recv.at[n], other)
        here = pltpu.make_async_copy(src, dst.at[core], dp_local.at[n])
        here.start()
        copies.append((there, here))

    def in_wait(n):
        dst = moved[n][1]
        for side in range(2):
            ref = dst.at[pl.ds(side * HALF, HALF)]

            @pl.when(owners[side] != me)
            def _():
                arrived(ref, in_send.at[n, 0], in_recv.at[n, side], {"ctx": owners[side]})

            @pl.when(owners[side] == me)
            def _():
                pltpu.make_async_copy(ref, ref, in_local.at[n]).wait()

    def dp_wait(n):
        copies[n][1].wait()
        arrived(weights[n][1].at[1 - core], dp_send.at[n], dp_recv.at[n], other)

    in_wait(0)
    in_wait(1)
    dp_wait(0)
    gain1 = jnp.concatenate([gains[0, 0:1, 0:288], gains[1, 0:1, 0:288]], axis=1)
    gain2 = jnp.concatenate([gains[0, 1:2, 0:288], gains[1, 1:2, 0:288]], axis=1)
    x = xz[...].astype(F32)
    h1f, _ = rms_forward(x, gain1)
    h1 = h1f.astype(BF16)
    h1_kept[...] = h1
    for n in (1, 2):
        dp_wait(n)

    def whole(ref):
        return ref[...].reshape(D, ref.shape[-1])

    cosines, sines = trig[:, 0:HEAD], trig[:, HEAD : 2 * HEAD]
    k_lin = nn(h1, whole(wk))
    v_lin = nn(h1, whole(wv))
    for h in every:
        cols = slice(h * HEAD, (h + 1) * HEAD)
        key = k_lin[:, cols]
        key = key * cosines + swap_halves(key) * sines
        kv[h, place.at[2], place.at[1], place.at[0]] = jnp.concatenate([key, v_lin[:, cols]], axis=1).astype(BF16)
    keys_gather = gather_task(place, kv, 0, ROWS, as_, ar)
    next(keys_gather)
    dp_wait(3)
    q_lin = nn(h1, whole(wq))
    for h in range(HEADS):
        query = q_lin[:, h * HEAD : (h + 1) * HEAD]
        query = (query * cosines + swap_halves(query) * sines).astype(BF16)
        query = (query.astype(F32) * HEAD**-0.5).astype(BF16)
        query = jnp.concatenate([query, jnp.zeros((ROWS, HEAD), BF16)], axis=1)
        group = (h % GROUPS) * HALF
        qpad[h // GROUPS, group : group + HALF] = query[:HALF]
        qpad[h // GROUPS, 192 + group : 192 + group + HALF] = query[HALF:]
    for _ in range(4):
        next(keys_gather)

    slab = place.at[2]
    inner = lax.rem(me, 16)
    late_rows = slice(192, 384)

    def spot(h, p, z, piece, side):
        rows = slice(side * HALF, (side + 1) * HALF)
        if h == 0:
            return (0, z, pl.ds(2 * piece, 2), slice(None), rows)
        if h == 1:
            return (1, z, slice(None), place.coord(0, p), rows)
        return (2, z, place.coord(1, p), slice(None), rows)

    def keys_at(h, p, z, piece, side):
        block = kv[spot(h, p, z, piece, side)]
        return block.reshape(-1, 128)

    def masks(h, p, piece):
        count = 512 if h == 0 else 256
        row = lax.broadcasted_iota(jnp.int32, (count, 384), 0)
        lane = lax.broadcasted_iota(jnp.int32, (count, 384), 1)
        block = row // HALF
        if h == 0:
            block = block + 8 * piece
        elif h == 1:
            block = 4 * block + place.coord(0, p)
        else:
            block = block + 4 * place.coord(1, p)
        token, query = lax.rem(row, HALF), lax.rem(lane, HALF)
        low = token + HALF * block <= jnp.where(lane < 192, HALF * inner + query, HALF * 64)
        high = token - HALF * block <= query - HALF * inner
        return low, high[:, :192]

    def by_plane(p, heads_of, others=None):
        def slabs(z, units):
            for kind, when in ((0, z < slab), (1, z == slab), (2, z > slab)):

                @pl.when(when)
                def _():
                    heads_of(units, z, kind)

        def one(z, _):
            slabs(z, ((1, 0), (2, 0)))
            return 0

        if p == 0:
            for piece in range(2):
                heads_of(((0, piece),), slab, 1)
        else:
            z = place.coord(2, p)
            for kind, when in ((0, z < slab), (2, z > slab)):

                @pl.when(when)
                def _():
                    heads_of(((0, 0), (0, 1)), z, kind)

        if others is None:
            lax.fori_loop(0, 4, one, 0)
        else:
            others()

    def forward_step(block, queries, mask, state):
        top, accum = state
        scores = nt(block, queries)
        if mask is not None:
            scores = jnp.where(mask, scores, MASKED)
        new_top = jnp.maximum(top, jnp.max(scores, axis=0, keepdims=True))
        weights = jnp.exp(scores - new_top).astype(BF16)
        ones_lane = lax.broadcasted_iota(jnp.int32, block.shape, 1) < HEAD
        values = jnp.where(ones_lane, jnp.ones_like(block), block)
        return new_top, accum * jnp.exp(top - new_top) + tn(values, weights)

    def forward_plane(p):
        def heads_of(units, z, kind):
            for h, piece in units:
                low, high = masks(h, p, piece) if kind == 1 else (None, None)
                if kind < 2:
                    state = (top_ab[h], acc_ab[h])
                    top_ab[h], acc_ab[h] = forward_step(keys_at(h, p, z, piece, 0), qpad[h], low, state)
                if kind > 0:
                    block = keys_at(h, p, z, piece, 1)
                    if kind == 2:
                        block = jnp.concatenate([keys_at(h, p, z, piece, 0), block], axis=0)
                    state = (top_b[h], acc_b[h])
                    top_b[h], acc_b[h] = forward_step(block, qpad[h, late_rows], high, state)

        def others():
            row = lax.broadcasted_iota(jnp.int32, (512, 384), 0)
            lane = lax.broadcasted_iota(jnp.int32, (512, 384), 1)
            token, query, block = lax.rem(row, HALF), lax.rem(lane, HALF), lax.rem(row // HALF, 4)
            for z in (0, 2):
                for h in (1, 2):
                    at = 4 * block + place.coord(0, p) if h == 1 else block + 4 * place.coord(1, p)
                    at = at + 16 * (row // 256)
                    ahead = HALF * (me - 16 * z)
                    low = token + HALF * at <= jnp.where(lane < 192, ahead + query, HALF * 128)
                    high = (token - HALF * at <= query - ahead)[:, :192]
                    early, late = (
                        jnp.concatenate([keys_at(h, p, z, 0, side), keys_at(h, p, z + 1, 0, side)], axis=0)
                        for side in range(2)
                    )
                    top_ab[h], acc_ab[h] = forward_step(early, qpad[h], low, (top_ab[h], acc_ab[h]))
                    top_b[h], acc_b[h] = forward_step(late, qpad[h, late_rows], high, (top_b[h], acc_b[h]))

        by_plane(p, heads_of, others)

    top_ab[...] = jnp.full_like(top_ab, MASKED)
    top_b[...] = jnp.full_like(top_b, MASKED)
    acc_ab[...] = jnp.zeros_like(acc_ab)
    acc_b[...] = jnp.zeros_like(acc_b)
    forward_plane(0)
    next(keys_gather)
    next(keys_gather)
    forward_plane(1)
    forward_plane(3)
    next(keys_gather)
    forward_plane(2)
    in_wait(2)
    for n in (4, 5, 6, 7):
        dp_wait(n)
    for h in every:
        top = jnp.maximum(top_ab[h][:, 192:], top_b[h])
        accum = acc_ab[h][:, 192:] * jnp.exp(top_ab[h][:, 192:] - top) + acc_b[h] * jnp.exp(top_b[h] - top)
        top = jnp.concatenate([top_ab[h][:, :192], top], axis=1)
        accum = jnp.concatenate([acc_ab[h][:, :192], accum], axis=1)
        total = accum[0:1, :]
        outs = accum / total
        outs_t[h] = outs
        lse[h] = top + jnp.log(total)
        attn[h] = outs.T.astype(BF16)

    def by_token(ref, lanes):
        pieces = []
        for h in range(HEADS):
            group = (h % GROUPS) * HALF
            here = ref[h // GROUPS]
            pieces.append(jnp.concatenate([here[group : group + HALF, lanes], here[192 + group : 192 + group + HALF, lanes]], axis=0))
        return jnp.concatenate(pieces, axis=1)

    attn_low = by_token(attn, slice(64, 128))

    def put(buf, rows, base, length, value, half):
        for tile in range(value.shape[1] // 128):
            at, done = base + tile * length, 0
            while done < value.shape[0]:
                chunk, row = (at + done) // rows, (at + done) % rows
                size = min(rows - row, value.shape[0] - done)
                spot = (chunk // 4 % 4, chunk % 4, slice(row, row + size))
                if len(buf.shape) == 7:
                    spot = (chunk // 64, chunk // 16 % 4, *spot)
                buf[(half, *spot)] = value[done : done + size, tile * 128 : (tile + 1) * 128].astype(BF16)
                done += size

    def gain_line(grad, half):
        line = jnp.concatenate([grad[:, 288 * half : 288 * (half + 1)], jnp.zeros((1, 96), F32)], axis=1)
        return jnp.concatenate([line[:, 128 * k : 128 * (k + 1)] for k in range(3)] + [jnp.zeros((13, 128), F32)], axis=0)

    x2 = x + nn(attn_low, whole(wo))
    h2f, inverse2 = rms_forward(x2, gain2)
    h2 = h2f.astype(BF16)
    pad = jnp.zeros((ROWS, 64), BF16)
    dy_low = cotz[...]
    total = x2
    grad_h2 = jnp.zeros((ROWS, D), F32)
    for t in range(2):
        cols = slice(768 * t, 768 * (t + 1))
        wg_t, wu_t = wg[:, :, cols].reshape(D, 768), wu[:, :, cols].reshape(D, 768)
        gate = nn(h2, wg_t)
        up = nn(h2, wu_t)
        sigma = jax.nn.sigmoid(gate)
        active = gate * sigma
        hidden = (active * up).astype(BF16)
        total = total + nt(hidden, wd[t])
        grad_hidden = nn(dy_low, wd[t])
        grad_gate = (grad_hidden * up * (sigma + active * (1.0 - sigma))).astype(BF16)
        grad_up = (grad_hidden * active).astype(BF16)
        grad_h2 = grad_h2 + nt(grad_gate, wg_t) + nt(grad_up, wu_t)
        for base, value in ((E_GATE, tn(h2, grad_gate)), (E_UP, tn(h2, grad_up))):
            for half in range(2):
                put(e_all, 64, base + 6 * t * 288, 288, value[288 * half : 288 * (half + 1)], half)
        put(e_all, 64, E_DOWN, 576, tn(dy_low, hidden), t)
    for part in range(2):
        send(e_all.at[1 - core, part], e_peer.at[part], dps.at[part], dpr.at[part], other)
    result[...] = total.astype(BF16)
    grad_norm2, grad_gain2 = rms_backward(x2, inverse2, gain2, grad_h2)
    grad_x2 = dy_low.astype(F32) + grad_norm2
    grad_x2_kept[...] = grad_x2
    grad_attn = grad_x2.astype(BF16)
    grad_out = tn(attn_low, jnp.concatenate([grad_attn, pad], axis=1))
    for half in range(2):
        put(e_all, 64, E_OUT, 288, grad_out[288 * half : 288 * (half + 1)], half)
        put(e_all, 64, E_GAIN, 16, gain_line(grad_gain2, half), half)
        put(e_all, 64, E_GAIN + 16, 0, jnp.zeros((E_ROWS - E_GAIN - 16, 128), F32), half)
    send(e_all.at[1 - core, 2], e_peer.at[2], dps.at[2], dpr.at[2], other)

    def out_copy(n, side, here=False):
        src, dst = ((result, out_result), (grad_z, out_grad))[n]
        k = lax.rem((me, 127 - me)[side], 2)
        a = src.at[pl.ds(side * HALF, HALF)]
        b = dst.at[pl.ds(pl.multiple_of(k * HALF, HALF), HALF)]
        if here:
            return pltpu.make_async_copy(a, b, zl.at[n])
        return remote(a, b, zs.at[n, side], zr.at[n, k], {"ctx": owners[side]})

    def out_send(n):
        for side in range(2):

            @pl.when(owners[side] != me)
            def _():
                out_copy(n, side).start()

            @pl.when(owners[side] == me)
            def _():
                out_copy(n, side, here=True).start()

    def out_wait(n):
        dst = (out_result, out_grad)[n]
        for k in range(2):
            ref = dst.at[pl.ds(k * HALF, HALF)]

            @pl.when(targets[k] != me)
            def _():
                arrived(ref, zs.at[n, 0], zr.at[n, k], {"ctx": targets[k]})

            @pl.when(targets[k] == me)
            def _():
                pltpu.make_async_copy(ref, ref, zl.at[n]).wait()

        for side in range(2):

            @pl.when(owners[side] != me)
            def _():
                out_copy(n, side).wait_send()

    out_send(0)
    e_work = e_all.at[core]

    def early():
        for part in range(3):
            remote(e_all.at[1 - core, part], e_peer.at[part], dps.at[part], dpr.at[part], other).wait()
            for z in range(4):
                index = (core, part, z)
                e_all[index] = (e_all[index].astype(F32) + e_peer[part, z].astype(F32)).astype(BF16)

        def e_keep(part, index, total):
            e_sum[index] = total.astype(BF16)

        yield from scatter_task(place, e_work, (eh0, eh1, eh2), (ew0, ew1, ew2), 64, es, er, e_keep)
        yield from gather_task(place, e_sum, 0, 64, gs, gr)

    early_task = early()

    grad_o = nt(grad_attn, whole(wo)).astype(BF16)
    for h in range(HEADS):
        piece = grad_o[:, h * HEAD : (h + 1) * HEAD]
        piece = jnp.concatenate([jnp.zeros((ROWS, HEAD), BF16), piece], axis=1)
        group = (h % GROUPS) * HALF
        dopad[h // GROUPS, group : group + HALF] = piece[:HALF]
        dopad[h // GROUPS, 192 + group : 192 + group + HALF] = piece[HALF:]

    deltas = [jnp.sum(dopad[h].astype(F32).T * outs_t[h], axis=0, keepdims=True) for h in every]
    logs = [lse[h] for h in every]

    def backward_step(block, queries, grads, log_total, delta, mask, grad_q):
        scores = nt(block, queries)
        if mask is not None:
            scores = jnp.where(mask, scores, MASKED)
        probs = jnp.exp(scores - log_total)
        grad_scores = (probs * (nt(block, grads) - delta)).astype(BF16)
        part = nn(grad_scores, queries) + nn(probs.astype(BF16), grads)
        return grad_q + tn(block, grad_scores), part.astype(BF16)

    dq_early[...] = jnp.zeros_like(dq_early)
    dq_late[...] = jnp.zeros_like(dq_late)

    def backward_plane(p):
        def heads_of(units, z, kind):
            for h, piece in units:
                low, high = masks(h, p, piece) if kind == 1 else (None, None)
                early_spot, late_spot = (spot(h, p, z, piece, side) for side in range(2))

                def save(at, part):
                    dkv[at] = part.reshape(-1, 4, HALF, 128) if h == 0 else part.reshape(4, HALF, 128)

                if kind < 2:
                    block = keys_at(h, p, z, piece, 0)
                    dq_early[h], part = backward_step(block, qpad[h], dopad[h], logs[h], deltas[h], low, dq_early[h])
                    save(early_spot, part)
                if kind == 0:
                    save(late_spot, jnp.zeros_like(part))
                else:
                    block = keys_at(h, p, z, piece, 1)
                    size = block.shape[0]
                    if kind == 2:
                        block = jnp.concatenate([keys_at(h, p, z, piece, 0), block], axis=0)
                    dq_late[h], part = backward_step(
                        block, qpad[h, late_rows], dopad[h, late_rows], logs[h][:, 192:], deltas[h][:, 192:],
                        high, dq_late[h],
                    )
                    if kind == 2:
                        save(early_spot, part[:size])
                        part = part[size:]
                    save(late_spot, part)

        by_plane(p, heads_of)

    def keep(part, index, total):
        own[part] = total

    keys_task = scatter_task(place, dkv, (kh0, kh1, kh2), (kw0, kw1, kw2), ROWS, ks, kr, keep, stepwise=True)
    backward_plane(2)
    next(keys_task)
    next(early_task)
    backward_plane(1)
    next(early_task)
    backward_plane(3)
    next(keys_task)
    next(early_task)
    next(keys_task)
    backward_plane(0)
    next(early_task)
    for h in every:
        dq_rows[h] = jnp.concatenate([dq_early[h][:, :192], dq_early[h][:, 192:] + dq_late[h]], axis=1).T
    grad_q = by_token(dq_rows, slice(0, 64)) * HEAD**-0.5
    pieces = []
    for h in range(HEADS):
        piece = grad_q[:, h * HEAD : (h + 1) * HEAD]
        pieces.append(piece * cosines - swap_halves(piece) * sines)
    dq_low = jnp.concatenate(pieces, axis=1).astype(BF16)
    grad_query = tn(h1_kept[...], jnp.concatenate([dq_low, pad], axis=1))
    for half in range(2):
        put(m_full, 96, 0, 288, grad_query[288 * half : 288 * (half + 1)], half)
        put(m_full, 96, 1440, 0, jnp.zeros((96, 128), F32), half)
    m_copy = send(m_full.at[1 - core], m_peer, dps.at[3], dpr.at[3], other)
    grad_h1_q = nt(dq_low, whole(wq))

    def middle_part():
        yield
        arrived(m_peer, dps.at[3], dpr.at[3], other)
        m_work[...] = (m_full[core].astype(F32) + m_peer[...].astype(F32)).astype(BF16)
        yield from plane_sum_task(place, m_work, m_slots, m_layers, m_sum, (m0, m1, m2, m3, m4, m5))
        m_copy.wait_send()

    def late_part():
        yield from keys_task
        keys, values = [], []
        for h in every:
            piece = own[h]
            grad_k = piece[:, :HEAD]
            keys.append(grad_k * cosines - swap_halves(grad_k) * sines)
            values.append(piece[:, HEAD:])
        dk_low = jnp.concatenate(keys, axis=1).astype(BF16)
        dv_low = jnp.concatenate(values, axis=1).astype(BF16)
        weight_grads = tn(h1_kept[...], jnp.concatenate([dk_low, dv_low], axis=1))
        grad_h1 = grad_h1_q + nt(dk_low, whole(wk)) + nt(dv_low, whole(wv))
        x = xz[...].astype(F32)
        inverse1 = lax.rsqrt(jnp.mean(x * x, axis=-1, keepdims=True) + EPS)
        grad_norm1, grad_gain1 = rms_backward(x, inverse1, gain1, grad_h1)
        for half in range(2):
            put(l_full, 64, 0, 288, weight_grads[288 * half : 288 * (half + 1)], half)
            put(l_full, 64, 864, 16, gain_line(grad_gain1, half), half)
            put(l_full, 64, 880, 0, jnp.zeros((144, 128), F32), half)
        l_copy = send(l_full.at[1 - core], l_peer, dps.at[4], dpr.at[4], other)
        grad_z[...] = (grad_x2_kept[...] + grad_norm1).astype(BF16)
        out_send(1)
        yield
        arrived(l_peer, dps.at[4], dpr.at[4], other)
        l_work[...] = (l_full[core].astype(F32) + l_peer[...].astype(F32)).astype(BF16)
        yield from plane_sum_task(place, l_work, l_slots, l_layers, l_sum, (l0, l1, l2, l3, l4, l5))
        l_copy.wait_send()

    run_together(late_part(), early_task, middle_part(), keys_gather)
    out_wait(0)
    out_wait(1)
    for there, _ in copies:
        there.wait_send()
    for n in range(3):
        for k in range(2):

            @pl.when(targets[k] != me)
            def _():
                in_copy(n, k).wait_send()


def layer_call(x, trig, cot, gain1, gain2, weights):
    def buffers(rows):
        dims = ((4, 4), (4,), ())
        halves = [pltpu.VMEM((3, 2, *d, rows // 2, 128), BF16) for d in dims]
        wholes = [pltpu.VMEM((3, 2, *d, rows, 128), BF16) for d in dims]
        return halves + wholes

    def summed(rows):
        dims = ((2, 4, 4), (4, 4), (4, 4), (15,), (4,))
        return [pltpu.VMEM((*d, rows, 128), BF16) for d in dims]

    sem = pltpu.SemaphoreType.DMA
    v = pltpu.VMEM
    return pl.pallas_call(
        layer_kernel,
        out_shape=(
            shape((3, 4, 4, 4, 64, 128), BF16), shape((4, 4, 96, 128), BF16), shape((4, 4, 64, 128), BF16),
            shape((ROWS, D), BF16), shape((ROWS, D), BF16),
        ),
        in_specs=(*vmem(5), *anywhere(7)),
        out_specs=tuple(vmem(5)),
        scratch_shapes=[
            v((ROWS, D), BF16), v((ROWS, D), BF16), v((8, 384), F32),
            v((ROWS, D), BF16), v((ROWS, 128), F32), v((ROWS, D), BF16), v((2, 8, 384), F32),
            *[v((2, *w.shape), BF16) for w in weights],
            v((ROWS, D), BF16), v((KV_HEADS, 384, 128), BF16), v((KV_HEADS, 4, 4, 4, ROWS, 128), BF16),
            v((KV_HEADS, 1, 384), F32), v((KV_HEADS, 128, 384), F32), v((KV_HEADS, 1, 192), F32), v((KV_HEADS, 128, 192), F32),
            v((KV_HEADS, 128, 384), F32), v((KV_HEADS, 1, 384), F32), v((KV_HEADS, 384, 128), BF16),
            v((KV_HEADS, 384, 128), BF16), v((KV_HEADS, 128, 384), F32), v((KV_HEADS, 128, 192), F32),
            v((KV_HEADS, 384, 128), F32), v((ROWS, D), BF16), v((ROWS, D), F32),
            v((3, 4, 4, 4, ROWS, 128), BF16), v((2, 3, 4, 4, 4, 64, 128), BF16), v((3, 4, 4, 4, 64, 128), BF16),
            *summed(96), *summed(64),
            v((3, ROWS, 128), F32), v((ROWS, D), BF16),
            *buffers(ROWS), *buffers(64),
            sem((3, 2)), sem((3, 2)), sem((3,)), sem((8,)), sem((8,)), sem((8,)), sem((3, 3, 6)), sem((3, 3, 6)),
            sem((3, 3, 6)), sem((3, 3, 6)), sem((3, 3, 6)), sem((3, 3, 6)), sem((3, 3, 6)), sem((3, 3, 6)),
            *[sem((n,)) for n in (15, 15, 3, 3, 15, 15) * 2],
            sem((5,)), sem((5,)), sem((2, 2)), sem((2, 2)), sem((2,)),
        ],
        compiler_params=pltpu.CompilerParams(collective_id=0, has_side_effects=True, vmem_limit_bytes=VMEM_LIMIT),
        name="decoder_layer",
    )(x, trig, cot, gain1, gain2, *weights)


def unpack_kernel(e, m, l, result, grad, result_t, grad_t, gain1, gq, gk, gv, go, gain2, gg, gu, gd):
    def take(ref, base, length, out):
        columns = out.shape[1]
        for tile in range(-(-columns // 128)):
            wide = min(128, columns - 128 * tile)
            at = base + tile * length
            out[:, 128 * tile : 128 * tile + wide] = ref[at : at + length, :wide].astype(F32)

    take(e, E_GATE, 288, gg)
    take(e, E_UP, 288, gu)
    take(e, E_DOWN, 576, gd)
    result_t[...] = result[...].T
    grad_t[...] = grad[...].T
    take(e, E_OUT, 288, go)
    take(m, 0, 288, gq)
    whole = jnp.concatenate([l[tile * 288 : (tile + 1) * 288, :] for tile in range(3)], axis=1).astype(F32)
    gk[...] = whole[:, 0:192]
    gv[...] = whole[:, 192:384]
    for ref, at, gain in ((e, E_GAIN, gain2), (l, 864, gain1)):
        lines = ref[at : at + 16, :].astype(F32)
        gain[...] = jnp.concatenate([lines[k : k + 1, :] for k in range(3)], axis=1)[:, :288].reshape(288)


def unpack_call(e, m, l, result, grad):
    return pl.pallas_call(
        unpack_kernel,
        out_shape=(
            shape((D, ROWS), BF16), shape((D, ROWS), BF16),
            shape((288,), F32), shape((288, D), F32), shape((288, 192), F32), shape((288, 192), F32),
            shape((288, D), F32), shape((288,), F32), shape((288, FF), F32), shape((288, FF), F32), shape((D, 768), F32),
        ),
        in_specs=vmem(5),
        out_specs=tuple(vmem(11)),
        compiler_params=pltpu.CompilerParams(vmem_limit_bytes=VMEM_LIMIT),
        name="unpack_gradients",
    )(e, m, l, result, grad)


def body(
    layer_in, positions, norm_gain1, w_query, w_key, w_value, w_out, norm_gain2, w_gate, w_up, w_down, cotangent
):
    inv_freq = np.tile(10000.0 ** (-np.arange(HEAD // 2) / (HEAD // 2)), 4).astype(np.float32)
    angles = positions[0].astype(F32)[:, None] * inv_freq[None, :]
    lane = lax.broadcasted_iota(jnp.int32, (ROWS, 128), 1)
    sines = jnp.sin(angles)
    trig = jnp.where(lane < 64, jnp.cos(angles), jnp.where(lane < 96, -sines, sines))
    e_sum, m_sum, l_sum, result, grad = layer_call(
        layer_in[0].T, trig, cotangent[0].T, norm_gain1, norm_gain2,
        (w_query, w_key, w_value, w_out, w_gate, w_up, w_down.T),
    )
    result, grad, gain1, gq, gk, gv, go, gain2, gg, gu, gd = unpack_call(
        e_sum.reshape(-1, 128), m_sum.reshape(-1, 128), l_sum.reshape(-1, 128), result, grad
    )
    return (result.T[None], grad.T[None], gain1, gq, gk, gv, go, gain2, gg, gu, gd.T)


def solution(mesh):
    weight = P("dp", None)
    tokens = P("dp", "ctx", None)
    return jax.shard_map(
        body,
        mesh=mesh,
        in_specs=(tokens, P("dp", "ctx"), P("dp"), weight, weight, weight, weight, P("dp"), weight, weight, weight, tokens),
        out_specs=(tokens, tokens, P("dp"), weight, weight, weight, weight, P("dp"), weight, weight, weight),
        check_vma=False,
    )
```
